128 devices in a mesh: section: 4 (over z_lo, core), dir: 2 (over z_hi), dp: 16 (over y, x).
Axes of the slice: x: 4, y: 4, z: 4 (z_hi: 2, z_lo: 2; z = z_hi * 2 + z_lo), core: 2. Of those that a mesh axis runs over, the one named last changes fastest.
Arguments:
- acts: bfloat16 [2, 4, 2048, 4096], P('dir', 'section', 'dp'), may hold values from -6 to 6
- top_cot: bfloat16 [2, 2048, 4096], P('dir', 'dp'), may hold values from -3 to 3
- weights: bfloat16 [2, 4, 4096, 2048], P('dir', 'section', 'dp'), may hold values from -0.09375 to 0.09375
- gains: float32 [4, 4096], replicated, may hold values from 0.1 to 1.9
Outputs:
- grad_w: float32 [2, 4, 4096, 2048], P('dir', 'section', 'dp')
- out_cot: bfloat16 [2, 4, 2048, 4096], P('dir', 'section', 'dp')
The draws below stay inside these ranges and needn't reach their ends.
All inputs are finite; a program needn't handle non-finite values.
Results may differ from the reference program's by a relative error of at most 0.02.
Values may be sent and summed in bfloat16 or wider, within the bound.
A program may use at most 192 MiB of HBM per device.

```python
import jax
import jax.numpy as jnp
from jax import lax

D = 4096
HALF = 2048
MICRO = 4
MB = 32
ROWS = 2048
N_SECTION = 4
N_DP = 16


def block_levels(key, dims, shards, smallest, high):
    loudness = 1.0
    for dim, parts in shards:
        draws = jax.random.uniform(jax.random.fold_in(jax.random.fold_in(key, 6), dim), (parts,), jnp.float32, smallest / len(shards), high / len(shards))
        loudness = loudness * jnp.repeat(jnp.exp(draws), dims[dim] // parts).reshape((-1,) + (1,) * (len(dims) - 1 - dim))
    return loudness


def gaussian(own_key, shape, width, bound, pieces=(), kind=jnp.bfloat16):
    result = width * jax.random.normal(own_key, shape, jnp.float32)
    if pieces:
        result = result * block_levels(own_key, shape, pieces, -0.22, 0.18)
    return jnp.clip(result, -bound, bound).astype(kind)


def setup_inputs(seed: int = 0) -> dict:
    keys = jax.random.split(jax.random.key(seed), 5)
    acts = gaussian(keys[0], (2, N_SECTION, ROWS, D), 1.0, 6.0, ((0, 2), (1, 4), (2, 16)))
    top_cot = gaussian(keys[1], (2, ROWS, D), 0.2, 3.0, ((0, 2), (1, 16)))
    weights = gaussian(keys[2], (2, N_SECTION, D, HALF), D ** -0.5, 0.09375, ((0, 2), (1, 4), (2, 16)))
    gains = jnp.clip(1.0 + 0.18 * jax.random.normal(keys[3], (N_SECTION, D), jnp.float32), 0.1, 1.9)
    return dict(acts=acts, top_cot=top_cot, weights=weights, gains=gains)


def slope_of(value):
    sig = jax.nn.sigmoid(value)
    return sig * (1.0 + value * (1.0 - sig))

def reference(acts, top_cot, weights, gains):
    half = D // 2
    layers = N_SECTION
    full = [jnp.concatenate([weights[0, l], weights[1, layers - 1 - l]], axis=1) for l in range(layers)]
    cot_out = [[None] * layers, [None] * layers]
    stored = {}
    for side in range(2):
        cot = top_cot[side]
        for depth in range(layers):
            l = layers - 1 - depth
            place = l if side == 0 else depth
            xf = acts[side, place].astype(jnp.float32)
            scale = lax.rsqrt(lax.optimization_barrier(jnp.mean(xf * xf, axis=-1, keepdims=True)) + 1e-05)
            normed = xf * scale
            hn = (normed * gains[l]).astype(jnp.bfloat16)
            w = full[l]
            u_low = jnp.dot(hn, w, preferred_element_type=jnp.float32).astype(jnp.bfloat16)
            u_val = lax.optimization_barrier(u_low).astype(jnp.float32)
            du = (cot.astype(jnp.float32) * slope_of(u_val)).astype(jnp.bfloat16)
            part_a = jnp.dot(du[:, :half], w[:, :half].T, preferred_element_type=jnp.float32).astype(jnp.bfloat16)
            part_b = jnp.dot(du[:, half:], w[:, half:].T, preferred_element_type=jnp.float32).astype(jnp.bfloat16)
            dhn = part_a.astype(jnp.float32) + part_b.astype(jnp.float32)
            dyn = dhn * gains[l]
            dxn = scale * (dyn - normed * lax.optimization_barrier(jnp.mean(dyn * normed, axis=-1, keepdims=True)))
            dx = (cot.astype(jnp.float32) + dxn).astype(jnp.bfloat16)
            cot_out[side][place] = dx
            stored[side, l] = (hn, du)
            cot = dx
    group_rows = MICRO * MB
    grads = []
    for l in range(layers):
        h_zero, d_zero = stored[0, l]
        h_one, d_one = stored[1, l]

        def one_group(g, total):
            start = (g * group_rows).astype(jnp.int32)
            ha = lax.dynamic_slice_in_dim(h_zero, start, group_rows, 0)
            da = lax.dynamic_slice_in_dim(d_zero, start, group_rows, 0)
            hb = lax.dynamic_slice_in_dim(h_one, start, group_rows, 0)
            db = lax.dynamic_slice_in_dim(d_one, start, group_rows, 0)
            term = jnp.dot(ha.T, da, preferred_element_type=jnp.float32) + jnp.dot(hb.T, db, preferred_element_type=jnp.float32)
            return total + term.astype(jnp.bfloat16).astype(jnp.float32)
        grads.append(lax.fori_loop(0, N_DP, one_group, jnp.zeros((D, D), jnp.float32)))
    grad_zero = jnp.stack([grads[l][:, :half] for l in range(layers)])
    grad_one = jnp.stack([grads[layers - 1 - p][:, half:] for p in range(layers)])
    grad_w = jnp.stack([grad_zero, grad_one])
    out_cot = jnp.stack([jnp.stack(cot_out[0]), jnp.stack(cot_out[1])])
    return (grad_w, out_cot)
```

```python
import functools

import jax
import jax.numpy as jnp
from jax import lax
from jax.experimental import pallas as pl
from jax.experimental.pallas import tpu as pltpu
from jax.sharding import PartitionSpec as P

MESH = pl.DeviceIdType.MESH
MICRO = 4
F32 = jnp.float32
BF16 = jnp.bfloat16


def wait_bytes(ref, sem):
    pltpu.make_async_copy(ref, ref, sem).wait()


def kernel(
    micro, side, layers,
    x_ref, top_ref, w_ref, gains_ref,
    grad_ref, out_ref,
    hns, hnb, wb, up, ur, c_own, c_oth, dxb, dyn_s, du, pr, pp, gp, gr, scl,
    s_w, r_w, s_hn, s_hp, r_hn, s_u, r_u, s_c, r_c, s_d, r_d, s_po, s_pp, r_p, s_g, r_g, s_top, s_t, s_out,
):
    mb, width = x_ref.shape[1], x_ref.shape[2]
    half = w_ref.shape[1]
    kc = w_ref.shape[0]
    kb = kc * side
    chunks = side * side
    h = lax.axis_index("dir")
    place = lax.axis_index("section")
    g = lax.axis_index("dp")
    layer = jnp.where(h == 0, place, layers - 1 - place)
    even = lax.rem(layer, 2) == 0
    gy, gx = lax.div(g, side), lax.rem(g, side)
    i, j = jnp.where(even, gy, gx), jnp.where(even, gx, gy)
    sa = jnp.where(even, side, 1)
    sb = jnp.where(even, 1, side)

    def where_is(l, d, a, b):
        return {"section": jnp.where(d == 0, l, layers - 1 - l), "dir": d, "dp": a * sa + b * sb}

    def at_layer(l, d):
        return {"section": jnp.where(d == 0, l, layers - 1 - l), "dir": d, "dp": g}

    def other(v, step):
        return lax.rem(v + step, side)

    def send(src, dst, s, r, to):
        pltpu.make_async_remote_copy(
            src_ref=src, dst_ref=dst, send_sem=s, recv_sem=r, device_id=to, device_id_type=MESH
        ).start()

    below = lax.rem(layer + layers - 1, layers)
    above = lax.rem(layer + 1, layers)
    first = layer == layers - 1
    last = layer == 0

    def chunk_of(q):
        a, b = q // side, q % side
        iq, jq = jnp.where(even, a, b), jnp.where(even, b, a)
        return iq, pl.ds(pl.multiple_of(jq * kc, kc), kc)

    peers = []
    for step in range(1, side):
        peers.append(where_is(layer, h, other(i, step), j))
        peers.append(where_is(layer, h, i, other(j, step)))
    for step in range(side):
        peers.append(where_is(layer, 1 - h, other(i, step), j))
    for l in (below, above):
        for d in (h, 1 - h):
            peers.append(at_layer(l, d))
    barrier = pltpu.get_barrier_semaphore()
    for to in peers:
        pl.semaphore_signal(barrier, inc=1, device_id=to, device_id_type=MESH)
    pl.semaphore_wait(barrier, len(peers))

    for step in (2, 1, 3) if side == 4 else range(1, side):
        send(w_ref, wb.at[j], s_w, r_w, where_is(layer, h, i, other(j, step)))
    pltpu.make_async_copy(w_ref, wb.at[j], r_w).start()

    @pl.when(first)
    def _():
        for m in range(micro):
            for n in range(2):
                pltpu.make_async_copy(
                    top_ref.at[m, :, pl.ds(n * half, half)], c_own.at[m, n], s_top
                ).start()

    gain_row = pl.ds(layer, 1)

    def norm_step(m, carry):
        xf = x_ref[m].astype(F32)
        scale = lax.rsqrt(jnp.mean(xf * xf, axis=-1, keepdims=True) + 1e-05)
        scl[m] = jnp.broadcast_to(scale, (mb, 128))
        for q in range(chunks):
            iq, cols = chunk_of(q)
            xq = x_ref[m, :, q * kc : (q + 1) * kc].astype(F32)
            hns[iq, m, :, cols] = (xq * scale * gains_ref[gain_row, q * kc : (q + 1) * kc]).astype(BF16)
        return carry

    lax.fori_loop(0, micro, norm_step, 0)
    for step in range(side):
        to = other(i, step)
        send(hns.at[to], hnb.at[:, i, h], s_hp, r_hn, where_is(layer, 1 - h, to, j))
        if step:
            send(hns.at[to], hnb.at[:, i, h], s_hn, r_hn, where_is(layer, h, to, j))
        else:
            pltpu.make_async_copy(hns.at[i], hnb.at[:, i, h], r_hn).start()

    @pl.when(first)
    def _():
        wait_bytes(c_own, s_top)
        for m in range(micro):
            send(c_own.at[m, 1 - h], c_oth.at[m], s_t.at[m], r_c.at[m, 1], at_layer(layer, 1 - h))

    wait_bytes(wb, r_w)
    wait_bytes(hnb, r_hn)

    tile = min(512, half)

    def fwd_step(m, carry):
        rows = hnb[m].reshape(side * 2 * mb, kb)
        for n in range(half // tile):
            cols = slice(n * tile, (n + 1) * tile)
            part = jnp.dot(rows, wb[:, :, cols].reshape(kb, tile), preferred_element_type=F32)
            up[m, :, :, :, cols] = part.astype(BF16).reshape(side, 2, mb, tile)
        for step in range(1, side):
            to = other(i, step)
            send(up.at[m, to], ur.at[m, i], s_u.at[m], r_u.at[m], where_is(layer, h, to, j))
        return carry

    lax.fori_loop(0, micro, fwd_step, 0)

    def du_step(m):
        wait_bytes(ur.at[m, pl.ds(0, side - 1)], r_u.at[m])

        @pl.when(jnp.logical_not(first))
        def _():
            wait_bytes(c_own.at[m], r_c.at[m, 0])

        wait_bytes(c_oth.at[m], r_c.at[m, 1])
        for n in range(half // tile):
            cols = slice(n * tile, (n + 1) * tile)
            for mine in range(2):
                r = h if mine else 1 - h
                u = up[m, i, r, :, cols].astype(F32)
                for step in range(1, side):
                    u = u + ur[m, other(i, step), r, :, cols].astype(F32)
                sig = jax.nn.sigmoid(u)
                slope = sig * (1.0 + u * (1.0 - sig))
                c = c_own[m, h, :, cols] if mine else c_oth[m, :, cols]
                du[m, i, r, :, cols] = (c.astype(F32) * slope).astype(BF16)
        for step in range(1, side):
            to = other(i, step)
            send(du.at[m, i], du.at[m, i], s_d.at[m], r_d.at[m], where_is(layer, h, to, j))

    def prod_step(m):
        wait_bytes(du.at[m, pl.ds(0, side - 1)], r_d.at[m])
        rows = du[m].reshape(side * 2 * mb, half)
        for k in range(side):
            part = lax.dot_general(rows, wb[k], (((1,), (1,)), ((), ())), preferred_element_type=F32)
            pr[m, :, :, :, k * kc : (k + 1) * kc] = part.astype(BF16).reshape(side, 2, mb, kc)
        for step in range(side):
            to = other(i, step)
            send(pr.at[m, to, 1 - h], pp.at[m, h, i], s_pp.at[m], r_p.at[m], where_is(layer, 1 - h, to, j))
            if step:
                send(pr.at[m, to, h], pp.at[m, h, i], s_po.at[m], r_p.at[m], where_is(layer, h, to, j))
            else:
                pltpu.make_async_copy(pr.at[m, i, h], pp.at[m, h, i], r_p.at[m]).start()

    def dx_step(m):
        wait_bytes(pp.at[m], r_p.at[m])
        scale = scl[m][:, :1]
        total = jnp.zeros((mb, kc), F32)
        for q in range(chunks):
            iq, cols = chunk_of(q)
            nat = slice(q * kc, (q + 1) * kc)
            dhn = pp[m, 0, iq, :, cols].astype(F32) + pp[m, 1, iq, :, cols].astype(F32)
            dyn = dhn * gains_ref[gain_row, nat]
            dyn_s[:, nat] = dyn
            total = total + dyn * (x_ref[m, :, nat].astype(F32) * scale)
        mean = jnp.sum(total, axis=-1, keepdims=True) * (1.0 / width)
        per = chunks // 2
        for q in range(chunks):
            nat = slice(q * kc, (q + 1) * kc)
            low = slice((q % per) * kc, (q % per + 1) * kc)
            normed = x_ref[m, :, nat].astype(F32) * scale
            dxn = scale * (dyn_s[:, nat] - normed * mean)
            dxb[m, q // per, :, low] = (c_own[m, q // per, :, low].astype(F32) + dxn).astype(BF16)

        @pl.when(jnp.logical_not(last))
        def _():
            send(dxb.at[m], c_own.at[m], s_c.at[m, 0], r_c.at[m, 0], at_layer(below, h))
            send(dxb.at[m, 1 - h], c_oth.at[m], s_c.at[m, 1], r_c.at[m, 1], at_layer(below, 1 - h))

        for n in range(2):
            pltpu.make_async_copy(dxb.at[m, n], out_ref.at[m, :, pl.ds(n * half, half)], s_out).start()

    def chain_step(t, carry):
        pl.when(t < micro)(lambda: du_step(t))
        pl.when((t >= 1) & (t < micro + 1))(lambda: prod_step(t - 1))
        pl.when(t >= 2)(lambda: dx_step(t - 2))
        return carry

    lax.fori_loop(0, micro + 2, chain_step, 0)

    def grad_block(b, n):
        cols = slice(n * tile, (n + 1) * tile)
        lhs = hnb[:, :, :, :, pl.ds(pl.multiple_of(b * kc, kc), kc)].reshape(micro * side * 2 * mb, kc)
        rhs = du[:, :, :, :, cols].reshape(micro * side * 2 * mb, tile)
        return lax.dot_general(lhs, rhs, (((0,), (0,)), ((), ())), preferred_element_type=F32)

    for slot, step in enumerate((2, 1, 3) if side == 4 else range(1, side)):
        to = other(j, step)
        for n in range(half // tile):
            gp[slot, :, n * tile : (n + 1) * tile] = grad_block(to, n).astype(BF16)
        send(gp.at[slot], gr.at[j], s_g, r_g, where_is(layer, h, i, to))
    for n in range(half // tile):
        grad_ref[:, n * tile : (n + 1) * tile] = grad_block(j, n)
    wait_bytes(gr.at[pl.ds(0, side - 1)], r_g)
    for n in range(half // tile):
        cols = slice(n * tile, (n + 1) * tile)
        total = grad_ref[:, cols]
        for step in range(1, side):
            total = total + gr[other(j, step), :, cols].astype(F32)
        grad_ref[:, cols] = total

    wait_bytes(wb.at[pl.ds(0, side - 1)], s_w)
    wait_bytes(hns.at[pl.ds(0, side - 1)], s_hn)
    wait_bytes(hns, s_hp)
    wait_bytes(gp, s_g)
    wait_bytes(dxb, s_out)

    def drain(m, carry):
        wait_bytes(up.at[m, pl.ds(0, side - 1)], s_u.at[m])
        wait_bytes(du.at[m, pl.ds(0, side - 1)], s_d.at[m])
        wait_bytes(pr.at[m, pl.ds(0, side - 1), 0], s_po.at[m])
        wait_bytes(pr.at[m, :, 0], s_pp.at[m])

        @pl.when(first)
        def _():
            wait_bytes(c_oth.at[m], s_t.at[m])

        @pl.when(jnp.logical_not(last))
        def _():
            wait_bytes(dxb.at[m], s_c.at[m, 0])
            wait_bytes(dxb.at[m, 0], s_c.at[m, 1])

        return carry

    lax.fori_loop(0, micro, drain, 0)


def shards(acts, top_cot, weights, gains):
    tokens, width = acts.shape[2], acts.shape[3]
    rows, half = weights.shape[2], weights.shape[3]
    layers = lax.axis_size("section")
    parts = lax.axis_size("dp")
    side = int(round(parts**0.5))
    micro = MICRO
    mb = tokens // micro
    kb = rows * side
    dma = pltpu.SemaphoreType.DMA
    vmem = pl.BlockSpec(memory_space=pltpu.VMEM)
    hbm = pl.BlockSpec(memory_space=pl.ANY)
    grad, out = pl.pallas_call(
        functools.partial(kernel, micro, side, layers),
        out_shape=(
            jax.ShapeDtypeStruct((rows, half), F32),
            jax.ShapeDtypeStruct((micro, mb, width), BF16),
        ),
        in_specs=[vmem, hbm, vmem, vmem],
        out_specs=(vmem, hbm),
        scratch_shapes=[
            pltpu.VMEM((side, micro, mb, kb), BF16),
            pltpu.VMEM((micro, side, 2, mb, kb), BF16),
            pltpu.VMEM((side, rows, half), BF16),
            pltpu.VMEM((micro, side, 2, mb, half), BF16),
            pltpu.VMEM((micro, side, 2, mb, half), BF16),
            pltpu.VMEM((micro, 2, mb, half), BF16),
            pltpu.VMEM((micro, mb, half), BF16),
            pltpu.VMEM((micro, 2, mb, half), BF16),
            pltpu.VMEM((mb, width), F32),
            pltpu.VMEM((micro, side, 2, mb, half), BF16),
            pltpu.VMEM((micro, side, 2, mb, kb), BF16),
            pltpu.VMEM((micro, 2, side, mb, kb), BF16),
            pltpu.VMEM((side - 1, rows, half), BF16),
            pltpu.VMEM((side, rows, half), BF16),
            pltpu.VMEM((micro, mb, 128), F32),
            dma, dma, dma, dma, dma,
            dma((micro,)), dma((micro,)),
            dma((micro, 2)), dma((micro, 2)),
            dma((micro,)), dma((micro,)),
            dma((micro,)), dma((micro,)), dma((micro,)),
            dma, dma, dma, dma((micro,)), dma,
        ],
        compiler_params=pltpu.CompilerParams(
            collective_id=0, has_side_effects=True, vmem_limit_bytes=60 * 1024 * 1024
        ),
        cost_estimate=pl.CostEstimate(
            flops=12 * tokens * width * half, bytes_accessed=8 * rows * half, transcendentals=0
        ),
    )(
        acts.reshape(micro, mb, width),
        top_cot.reshape(micro, mb, width),
        weights.reshape(rows, half),
        gains,
    )
    return grad[None, None], out.reshape(1, 1, tokens, width)


def solution(mesh):
    return jax.shard_map(
        shards,
        mesh=mesh,
        in_specs=(
            P("dir", "section", "dp", None),
            P("dir", "dp", None),
            P("dir", "section", "dp", None),
            P(),
        ),
        out_specs=(P("dir", "section", "dp", None), P("dir", "section", "dp", None)),
        check_vma=False,
    )
```

```python
import functools

import jax
import jax.numpy as jnp
from jax import lax
from jax.experimental import pallas as pl
from jax.experimental.pallas import tpu as pltpu
from jax.sharding import PartitionSpec as P

MESH = pl.DeviceIdType.MESH
MICRO = 8
F32 = jnp.float32
BF16 = jnp.bfloat16


def wait_bytes(ref, sem):
    pltpu.make_async_copy(ref, ref, sem).wait()


def kernel(
    micro, side, layers,
    x_ref, top_ref, w_ref, gains_ref,
    grad_ref, out_ref,
    hns, hnb, wb, up, ur, c_own, c_oth, dxb, dyn_s, du, pr, pp, gp, gr, scl,
    s_w, r_w, s_hn, s_hp, r_hn, s_u, r_u, s_c, r_c, s_d, r_d, s_po, s_pp, r_p, s_g, r_g, s_top, s_t, s_out, turn,
):
    mb, width = x_ref.shape[1], x_ref.shape[2]
    half = w_ref.shape[1]
    kc = w_ref.shape[0]
    kb = kc * side
    chunks = side * side
    h = lax.axis_index("dir")
    place = lax.axis_index("section")
    g = lax.axis_index("dp")
    layer = jnp.where(h == 0, place, layers - 1 - place)
    even = lax.rem(layer, 2) == 0
    gy, gx = lax.div(g, side), lax.rem(g, side)
    i, j = jnp.where(even, gy, gx), jnp.where(even, gx, gy)
    sa = jnp.where(even, side, 1)
    sb = jnp.where(even, 1, side)

    def where_is(l, d, a, b):
        return {"section": jnp.where(d == 0, l, layers - 1 - l), "dir": d, "dp": a * sa + b * sb}

    def at_layer(l, d):
        return {"section": jnp.where(d == 0, l, layers - 1 - l), "dir": d, "dp": g}

    def other(v, step):
        return lax.rem(v + step, side)

    def send(src, dst, s, r, to):
        pltpu.make_async_remote_copy(
            src_ref=src, dst_ref=dst, send_sem=s, recv_sem=r, device_id=to, device_id_type=MESH
        ).start()

    below = lax.rem(layer + layers - 1, layers)
    above = lax.rem(layer + 1, layers)
    first = layer == layers - 1
    last = layer == 0

    def chunk_of(q):
        a, b = q // side, q % side
        iq, jq = jnp.where(even, a, b), jnp.where(even, b, a)
        return iq, pl.ds(pl.multiple_of(jq * kc, kc), kc)

    peers = []
    for step in range(1, side):
        peers.append(where_is(layer, h, other(i, step), j))
        peers.append(where_is(layer, h, i, other(j, step)))
    for step in range(side):
        peers.append(where_is(layer, 1 - h, other(i, step), j))
    for l in (below, above):
        for d in (h, 1 - h):
            peers.append(at_layer(l, d))
    barrier = pltpu.get_barrier_semaphore()
    for to in peers:
        pl.semaphore_signal(barrier, inc=1, device_id=to, device_id_type=MESH)
    pl.semaphore_wait(barrier, len(peers))

    for step in (2, 1, 3) if side == 4 else range(1, side):
        send(w_ref, wb.at[j], s_w, r_w, where_is(layer, h, i, other(j, step)))
    pltpu.make_async_copy(w_ref, wb.at[j], r_w).start()

    @pl.when(first)
    def _():
        for m in range(micro):
            for n in range(2):
                pltpu.make_async_copy(
                    top_ref.at[m, :, pl.ds(n * half, half)], c_own.at[m, n], s_top
                ).start()

    gain_row = pl.ds(layer, 1)

    def norm_step(m, carry):
        xf = x_ref[m].astype(F32)
        scale = lax.rsqrt(jnp.mean(xf * xf, axis=-1, keepdims=True) + 1e-05)
        scl[m] = jnp.broadcast_to(scale, (mb, 128))
        for q in range(chunks):
            iq, cols = chunk_of(q)
            xq = x_ref[m, :, q * kc : (q + 1) * kc].astype(F32)
            hns[iq, m, :, cols] = (xq * scale * gains_ref[gain_row, q * kc : (q + 1) * kc]).astype(BF16)
        return carry

    lax.fori_loop(0, micro, norm_step, 0)
    for step in range(side):
        to = other(i, step)
        send(hns.at[to], hnb.at[:, i, h], s_hp, r_hn, where_is(layer, 1 - h, to, j))
        if step:
            send(hns.at[to], hnb.at[:, i, h], s_hn, r_hn, where_is(layer, h, to, j))
        else:
            pltpu.make_async_copy(hns.at[i], hnb.at[:, i, h], r_hn).start()

    @pl.when(first)
    def _():
        wait_bytes(c_own, s_top)
        for m in range(micro):
            send(c_own.at[m, 1 - h], c_oth.at[m], s_t.at[m], r_c.at[m, 1], at_layer(layer, 1 - h))

    wait_bytes(wb, r_w)
    wait_bytes(hnb, r_hn)

    tile = min(512, half)

    def fwd_step(m, carry):
        rows = hnb[m].reshape(side * 2 * mb, kb)
        for n in range(half // tile):
            cols = slice(n * tile, (n + 1) * tile)
            part = jnp.dot(rows, wb[:, :, cols].reshape(kb, tile), preferred_element_type=F32)
            up[m, :, :, :, cols] = part.astype(BF16).reshape(side, 2, mb, tile)
        for step in range(1, side):
            to = other(i, step)
            send(up.at[m, to], ur.at[m, i], s_u.at[m], r_u.at[m], where_is(layer, h, to, j))
        return carry

    lax.fori_loop(0, micro, fwd_step, 0)

    def du_step(m):
        wait_bytes(ur.at[m, pl.ds(0, side - 1)], r_u.at[m])

        @pl.when(jnp.logical_not(first))
        def _():
            wait_bytes(c_own.at[m], r_c.at[m, 0])

        wait_bytes(c_oth.at[m], r_c.at[m, 1])
        for n in range(half // tile):
            cols = slice(n * tile, (n + 1) * tile)
            for mine in range(2):
                r = h if mine else 1 - h
                u = up[m, i, r, :, cols].astype(F32)
                for step in range(1, side):
                    u = u + ur[m, other(i, step), r, :, cols].astype(F32)
                sig = jax.nn.sigmoid(u)
                slope = sig * (1.0 + u * (1.0 - sig))
                c = c_own[m, h, :, cols] if mine else c_oth[m, :, cols]
                du[m, i, r, :, cols] = (c.astype(F32) * slope).astype(BF16)
        for step in range(1, side):
            to = other(i, step)
            send(du.at[m, i], du.at[m, i], s_d.at[m], r_d.at[m], where_is(layer, h, to, j))

    def prod_step(m):
        wait_bytes(du.at[m, pl.ds(0, side - 1)], r_d.at[m])
        rows = du[m].reshape(side * 2 * mb, half)
        for k in range(side):
            part = lax.dot_general(rows, wb[k], (((1,), (1,)), ((), ())), preferred_element_type=F32)
            pr[m, :, :, :, k * kc : (k + 1) * kc] = part.astype(BF16).reshape(side, 2, mb, kc)
        for step in range(side):
            to = other(i, step)
            send(pr.at[m, to, 1 - h], pp.at[m, h, i], s_pp.at[m], r_p.at[m], where_is(layer, 1 - h, to, j))
            if step:
                send(pr.at[m, to, h], pp.at[m, h, i], s_po.at[m], r_p.at[m], where_is(layer, h, to, j))
            else:
                pltpu.make_async_copy(pr.at[m, i, h], pp.at[m, h, i], r_p.at[m]).start()

    def dx_step(m):
        wait_bytes(pp.at[m], r_p.at[m])
        scale = scl[m][:, :1]
        total = jnp.zeros((mb, kc), F32)
        for q in range(chunks):
            iq, cols = chunk_of(q)
            nat = slice(q * kc, (q + 1) * kc)
            dhn = pp[m, 0, iq, :, cols].astype(F32) + pp[m, 1, iq, :, cols].astype(F32)
            dyn = dhn * gains_ref[gain_row, nat]
            dyn_s[:, nat] = dyn
            total = total + dyn * (x_ref[m, :, nat].astype(F32) * scale)
        mean = jnp.sum(total, axis=-1, keepdims=True) * (1.0 / width)
        per = chunks // 2
        for q in range(chunks):
            nat = slice(q * kc, (q + 1) * kc)
            low = slice((q % per) * kc, (q % per + 1) * kc)
            normed = x_ref[m, :, nat].astype(F32) * scale
            dxn = scale * (dyn_s[:, nat] - normed * mean)
            dxb[m, q // per, :, low] = (c_own[m, q // per, :, low].astype(F32) + dxn).astype(BF16)

        @pl.when(jnp.logical_not(last))
        def _():
            send(dxb.at[m], c_own.at[m], s_c.at[m, 0], r_c.at[m, 0], at_layer(below, h))
            send(dxb.at[m, 1 - h], c_oth.at[m], s_c.at[m, 1], r_c.at[m, 1], at_layer(below, 1 - h))

        for n in range(2):
            pltpu.make_async_copy(dxb.at[m, n], out_ref.at[m, :, pl.ds(n * half, half)], s_out).start()

    def chain_step(t, carry):
        pl.when(t < micro)(lambda: du_step(t))
        pl.when((t >= 1) & (t < micro + 1))(lambda: prod_step(t - 1))
        pl.when(t >= 2)(lambda: dx_step(t - 2))
        return carry

    lax.fori_loop(0, micro + 2, chain_step, 0)

    def grad_block(b, n):
        cols = slice(n * tile, (n + 1) * tile)
        lhs = hnb[:, :, :, :, pl.ds(pl.multiple_of(b * kc, kc), kc)].reshape(micro * side * 2 * mb, kc)
        rhs = du[:, :, :, :, cols].reshape(micro * side * 2 * mb, tile)
        return lax.dot_general(lhs, rhs, (((0,), (0,)), ((), ())), preferred_element_type=F32)

    order = (2, 1, 3) if side == 4 else range(1, side)

    @pl.when(even)
    def _():
        pl.semaphore_signal(turn, inc=1, device_id=at_layer(above, h), device_id_type=MESH)

    for slot, step in enumerate(order):
        to = other(j, step)
        for n in range(half // tile):
            gp[slot, :, n * tile : (n + 1) * tile] = grad_block(to, n).astype(BF16)
        if slot == 0:
            pl.when(jnp.logical_not(even))(lambda: pl.semaphore_wait(turn, 1))
        send(gp.at[slot], gr.at[j], s_g, r_g, where_is(layer, h, i, to))
    for n in range(half // tile):
        grad_ref[:, n * tile : (n + 1) * tile] = grad_block(j, n)
    wait_bytes(gr.at[pl.ds(0, side - 1)], r_g)
    for n in range(half // tile):
        cols = slice(n * tile, (n + 1) * tile)
        total = grad_ref[:, cols]
        for step in range(1, side):
            total = total + gr[other(j, step), :, cols].astype(F32)
        grad_ref[:, cols] = total

    wait_bytes(wb.at[pl.ds(0, side - 1)], s_w)
    wait_bytes(hns.at[pl.ds(0, side - 1)], s_hn)
    wait_bytes(hns, s_hp)
    wait_bytes(gp, s_g)
    wait_bytes(dxb, s_out)

    def drain(m, carry):
        wait_bytes(up.at[m, pl.ds(0, side - 1)], s_u.at[m])
        wait_bytes(du.at[m, pl.ds(0, side - 1)], s_d.at[m])
        wait_bytes(pr.at[m, pl.ds(0, side - 1), 0], s_po.at[m])
        wait_bytes(pr.at[m, :, 0], s_pp.at[m])

        @pl.when(first)
        def _():
            wait_bytes(c_oth.at[m], s_t.at[m])

        @pl.when(jnp.logical_not(last))
        def _():
            wait_bytes(dxb.at[m], s_c.at[m, 0])
            wait_bytes(dxb.at[m, 0], s_c.at[m, 1])

        return carry

    lax.fori_loop(0, micro, drain, 0)


def shards(acts, top_cot, weights, gains):
    tokens, width = acts.shape[2], acts.shape[3]
    rows, half = weights.shape[2], weights.shape[3]
    layers = lax.axis_size("section")
    parts = lax.axis_size("dp")
    side = int(round(parts**0.5))
    micro = MICRO
    mb = tokens // micro
    kb = rows * side
    dma = pltpu.SemaphoreType.DMA
    vmem = pl.BlockSpec(memory_space=pltpu.VMEM)
    hbm = pl.BlockSpec(memory_space=pl.ANY)
    grad, out = pl.pallas_call(
        functools.partial(kernel, micro, side, layers),
        out_shape=(
            jax.ShapeDtypeStruct((rows, half), F32),
            jax.ShapeDtypeStruct((micro, mb, width), BF16),
        ),
        in_specs=[vmem, hbm, vmem, vmem],
        out_specs=(vmem, hbm),
        scratch_shapes=[
            pltpu.VMEM((side, micro, mb, kb), BF16),
            pltpu.VMEM((micro, side, 2, mb, kb), BF16),
            pltpu.VMEM((side, rows, half), BF16),
            pltpu.VMEM((micro, side, 2, mb, half), BF16),
            pltpu.VMEM((micro, side, 2, mb, half), BF16),
            pltpu.VMEM((micro, 2, mb, half), BF16),
            pltpu.VMEM((micro, mb, half), BF16),
            pltpu.VMEM((micro, 2, mb, half), BF16),
            pltpu.VMEM((mb, width), F32),
            pltpu.VMEM((micro, side, 2, mb, half), BF16),
            pltpu.VMEM((micro, side, 2, mb, kb), BF16),
            pltpu.VMEM((micro, 2, side, mb, kb), BF16),
            pltpu.VMEM((side - 1, rows, half), BF16),
            pltpu.VMEM((side, rows, half), BF16),
            pltpu.VMEM((micro, mb, 128), F32),
            dma, dma, dma, dma, dma,
            dma((micro,)), dma((micro,)),
            dma((micro, 2)), dma((micro, 2)),
            dma((micro,)), dma((micro,)),
            dma((micro,)), dma((micro,)), dma((micro,)),
            dma, dma, dma, dma((micro,)), dma,
            pltpu.SemaphoreType.REGULAR,
        ],
        compiler_params=pltpu.CompilerParams(
            collective_id=0, has_side_effects=True, vmem_limit_bytes=60 * 1024 * 1024
        ),
        cost_estimate=pl.CostEstimate(
            flops=12 * tokens * width * half, bytes_accessed=8 * rows * half, transcendentals=0
        ),
    )(
        acts.reshape(micro, mb, width),
        top_cot.reshape(micro, mb, width),
        weights.reshape(rows, half),
        gains,
    )
    return grad[None, None], out.reshape(1, 1, tokens, width)


def solution(mesh):
    return jax.shard_map(
        shards,
        mesh=mesh,
        in_specs=(
            P("dir", "section", "dp", None),
            P("dir", "dp", None),
            P("dir", "section", "dp", None),
            P(),
        ),
        out_specs=(P("dir", "section", "dp", None), P("dir", "section", "dp", None)),
        check_vma=False,
    )
```

```python
import functools

import jax
import jax.numpy as jnp
from jax import lax
from jax.experimental import pallas as pl
from jax.experimental.pallas import tpu as pltpu
from jax.sharding import PartitionSpec as P

MESH = pl.DeviceIdType.MESH
MICRO = 8
F32 = jnp.float32
BF16 = jnp.bfloat16


def wait_bytes(ref, sem):
    pltpu.make_async_copy(ref, ref, sem).wait()


def kernel(
    micro, side, layers,
    x_hbm, top_ref, w_hbm, gains_ref,
    own_ref, gr, out_ref,
    x_ref, hns, hnb, wb, up, ur, ul, c_own, c_oth, dxb, dyn_s, du, pr, pp, gp, gl, gown, scl,
    s_w, r_w, s_hn, s_hp, r_hn, s_u, r_u, r_ul, s_c, r_c, s_d, r_d, s_po, s_pp, r_p, s_g, r_g, r_gl, s_own, s_top, s_t, s_out, s_in, turn, ready,
):
    mb, width = x_ref.shape[1], x_ref.shape[2]
    half = w_hbm.shape[1]
    kc = w_hbm.shape[0]
    kb = kc * side
    chunks = side * side
    h = lax.axis_index("dir")
    place = lax.axis_index("section")
    g = lax.axis_index("dp")
    layer = jnp.where(h == 0, place, layers - 1 - place)
    even = lax.rem(layer, 2) == 0
    gy, gx = lax.div(g, side), lax.rem(g, side)
    i, j = jnp.where(even, gy, gx), jnp.where(even, gx, gy)
    sa = jnp.where(even, side, 1)
    sb = jnp.where(even, 1, side)

    def where_is(l, d, a, b):
        return {"section": jnp.where(d == 0, l, layers - 1 - l), "dir": d, "dp": a * sa + b * sb}

    def at_layer(l, d):
        return {"section": jnp.where(d == 0, l, layers - 1 - l), "dir": d, "dp": g}

    def other(v, step):
        return lax.rem(v + step, side)

    i_right, i_far, i_left = other(i, 1), other(i, 2), other(i, 3)
    j_right, j_far, j_left = other(j, 1), other(j, 2), other(j, 3)
    a_right, a_left = where_is(layer, h, i_right, j), where_is(layer, h, i_left, j)
    b_right, b_left = where_is(layer, h, i, j_right), where_is(layer, h, i, j_left)
    low, high = pl.ds(0, kc // 2), pl.ds(kc // 2, kc // 2)

    def send(src, dst, s, r, to):
        pltpu.make_async_remote_copy(
            src_ref=src, dst_ref=dst, send_sem=s, recv_sem=r, device_id=to, device_id_type=MESH
        ).start()

    below = lax.rem(layer + layers - 1, layers)
    above = lax.rem(layer + 1, layers)
    first = layer == layers - 1
    last = layer == 0

    def chunk_of(q):
        a, b = q // side, q % side
        iq, jq = jnp.where(even, a, b), jnp.where(even, b, a)
        return iq, pl.ds(pl.multiple_of(jq * kc, kc), kc)

    peers = []
    for step in range(1, side):
        peers.append(where_is(layer, h, other(i, step), j))
        peers.append(where_is(layer, h, i, other(j, step)))
    for step in range(side):
        peers.append(where_is(layer, 1 - h, other(i, step), j))
    for l in (below, above):
        for d in (h, 1 - h):
            peers.append(at_layer(l, d))
    barrier = pltpu.get_barrier_semaphore()
    for to in peers:
        pl.semaphore_signal(barrier, inc=1, device_id=to, device_id_type=MESH)
    load_x = pltpu.make_async_copy(x_hbm, x_ref, s_in.at[0])
    load_x.start()
    load_w = pltpu.make_async_copy(w_hbm, wb.at[j], s_in.at[1])
    load_w.start()

    @pl.when(first)
    def _():
        for m in range(micro):
            for n in range(2):
                pltpu.make_async_copy(
                    top_ref.at[m, :, pl.ds(n * half, half)], c_own.at[m, n], s_top
                ).start()

    gain_row = pl.ds(layer, 1)

    def norm_step(m, carry):
        xf = x_ref[m].astype(F32)
        scale = lax.rsqrt(jnp.mean(xf * xf, axis=-1, keepdims=True) + 1e-05)
        scl[m] = jnp.broadcast_to(scale, (mb, 128))
        for q in range(chunks):
            iq, cols = chunk_of(q)
            xq = x_ref[m, :, q * kc : (q + 1) * kc].astype(F32)
            hns[iq, m, :, cols] = (xq * scale * gains_ref[gain_row, q * kc : (q + 1) * kc]).astype(BF16)
        return carry

    load_x.wait()
    lax.fori_loop(0, micro, norm_step, 0)
    load_w.wait()
    pl.semaphore_wait(barrier, len(peers))

    def pass_w(slot, part, sem, to):
        send(wb.at[slot, part], wb.at[slot, part], s_w, r_w.at[sem], to)

    def got_w(slot, part, sem):
        wait_bytes(wb.at[slot, part], r_w.at[sem])

    pass_w(j, low, 0, b_right)
    pass_w(j, high, 2, b_left)
    pass_w(j, high, 1, b_right)
    pass_w(j, low, 3, b_left)

    def relay_w():
        got_w(j_left, low, 0)
        pass_w(j_left, low, 4, b_right)
        got_w(j_right, high, 2)
        pass_w(j_right, high, 5, b_left)

    @pl.when(even)
    def _():
        relay_w()
        pl.semaphore_wait(ready, 1)

    for step in range(side):
        to = other(i, step)
        send(hns.at[to], hnb.at[:, i, h], s_hp, r_hn, where_is(layer, 1 - h, to, j))
        if step:
            send(hns.at[to], hnb.at[:, i, h], s_hn, r_hn, where_is(layer, h, to, j))
        else:
            pltpu.make_async_copy(hns.at[i], hnb.at[:, i, h], r_hn).start()

    @pl.when(first)
    def _():
        wait_bytes(c_own, s_top)
        for m in range(micro):
            send(c_own.at[m, 1 - h], c_oth.at[m], s_t.at[m], r_c.at[m, 1], at_layer(layer, 1 - h))

    pl.when(jnp.logical_not(even))(relay_w)
    got_w(j_left, high, 1)
    got_w(j_right, low, 3)
    got_w(j_far, low, 4)
    got_w(j_far, high, 5)

    @pl.when(jnp.logical_not(even))
    def _():
        pl.semaphore_signal(ready, inc=1, device_id=at_layer(below, h), device_id_type=MESH)

    wait_bytes(hnb, r_hn)

    tile = min(512, half)

    def fwd_step(m):
        rows = hnb[m].reshape(side * 2 * mb, kb)
        for n in range(half // tile):
            cols = slice(n * tile, (n + 1) * tile)
            part = jnp.dot(rows, wb[:, :, cols].reshape(kb, tile), preferred_element_type=F32)
            up[m, :, :, :, cols] = part.astype(BF16).reshape(side, 2, mb, tile)
        send(up.at[m, i_far, 0], ul.at[m, 0], s_u.at[m], r_ul.at[m, 0], a_right)
        send(up.at[m, i_far, 1], ul.at[m, 1], s_u.at[m], r_ul.at[m, 1], a_left)
        send(up.at[m, i_right, 1], ur.at[m, 0, 1], s_u.at[m], r_u.at[m], a_right)
        send(up.at[m, i_left, 0], ur.at[m, 1, 0], s_u.at[m], r_u.at[m], a_left)

    def relay_step(m):
        for r, (to, dev) in enumerate(((i_right, a_right), (i_left, a_left))):
            wait_bytes(ul.at[m, r], r_ul.at[m, r])
            for n in range(half // tile):
                cols = slice(n * tile, (n + 1) * tile)
                part = up[m, to, r, :, cols].astype(F32) + ul[m, r, :, cols].astype(F32)
                up[m, to, r, :, cols] = part.astype(BF16)
            send(up.at[m, to, r], ur.at[m, r, r], s_u.at[m], r_u.at[m], dev)

    def du_step(m):
        wait_bytes(ur.at[m], r_u.at[m])

        @pl.when(jnp.logical_not(first))
        def _():
            wait_bytes(c_own.at[m], r_c.at[m, 0])

        wait_bytes(c_oth.at[m], r_c.at[m, 1])
        for n in range(half // tile):
            cols = slice(n * tile, (n + 1) * tile)
            for mine in range(2):
                r = h if mine else 1 - h
                u = up[m, i, r, :, cols].astype(F32)
                u = u + ur[m, 0, r, :, cols].astype(F32) + ur[m, 1, r, :, cols].astype(F32)
                sig = jax.nn.sigmoid(u)
                slope = sig * (1.0 + u * (1.0 - sig))
                c = c_own[m, h, :, cols] if mine else c_oth[m, :, cols]
                du[m, i, r, :, cols] = (c.astype(F32) * slope).astype(BF16)
        for step in range(1, side):
            to = other(i, step)
            send(du.at[m, i], du.at[m, i], s_d.at[m], r_d.at[m], where_is(layer, h, to, j))

    def prod_step(m):
        wait_bytes(du.at[m, pl.ds(0, side - 1)], r_d.at[m])
        rows = du[m].reshape(side * 2 * mb, half)
        for k in range(side):
            part = lax.dot_general(rows, wb[k], (((1,), (1,)), ((), ())), preferred_element_type=F32)
            pr[m, :, :, :, k * kc : (k + 1) * kc] = part.astype(BF16).reshape(side, 2, mb, kc)
        for step in range(side):
            to = other(i, step)
            send(pr.at[m, to, 1 - h], pp.at[m, h, i], s_pp.at[m], r_p.at[m], where_is(layer, 1 - h, to, j))
            if step:
                send(pr.at[m, to, h], pp.at[m, h, i], s_po.at[m], r_p.at[m], where_is(layer, h, to, j))
            else:
                pltpu.make_async_copy(pr.at[m, i, h], pp.at[m, h, i], r_p.at[m]).start()

    def dx_step(m):
        wait_bytes(pp.at[m], r_p.at[m])
        scale = scl[m][:, :1]
        total = jnp.zeros((mb, kc), F32)
        for q in range(chunks):
            iq, cols = chunk_of(q)
            nat = slice(q * kc, (q + 1) * kc)
            dhn = pp[m, 0, iq, :, cols].astype(F32) + pp[m, 1, iq, :, cols].astype(F32)
            dyn = dhn * gains_ref[gain_row, nat]
            dyn_s[:, nat] = dyn
            total = total + dyn * (x_ref[m, :, nat].astype(F32) * scale)
        mean = jnp.sum(total, axis=-1, keepdims=True) * (1.0 / width)
        per = chunks // 2
        for q in range(chunks):
            nat = slice(q * kc, (q + 1) * kc)
            low = slice((q % per) * kc, (q % per + 1) * kc)
            normed = x_ref[m, :, nat].astype(F32) * scale
            dxn = scale * (dyn_s[:, nat] - normed * mean)
            dxb[m, q // per, :, low] = (c_own[m, q // per, :, low].astype(F32) + dxn).astype(BF16)

        @pl.when(jnp.logical_not(last))
        def _():
            send(dxb.at[m], c_own.at[m], s_c.at[m, 0], r_c.at[m, 0], at_layer(below, h))
            send(dxb.at[m, 1 - h], c_oth.at[m], s_c.at[m, 1], r_c.at[m, 1], at_layer(below, 1 - h))

        for n in range(2):
            pltpu.make_async_copy(dxb.at[m, n], out_ref.at[m, :, pl.ds(n * half, half)], s_out).start()

    lag = 2
    begin = jnp.where(first, lag + 1, micro + lag)

    def step_at(t, carry):
        c = t - begin
        pl.when(t < micro)(lambda: fwd_step(t))
        pl.when((t >= lag) & (t < micro + lag))(lambda: relay_step(t - lag))
        pl.when((c >= 0) & (c < micro))(lambda: du_step(c))
        pl.when((c >= 1) & (c < micro + 1))(lambda: prod_step(c - 1))
        pl.when(c >= 2)(lambda: dx_step(c - 2))
        return carry

    lax.fori_loop(0, begin + micro + 2, step_at, 0)

    def grad_block(b, n):
        cols = slice(n * tile, (n + 1) * tile)
        lhs = hnb[:, :, :, :, pl.ds(pl.multiple_of(b * kc, kc), kc)].reshape(micro * side * 2 * mb, kc)
        rhs = du[:, :, :, :, cols].reshape(micro * side * 2 * mb, tile)
        return lax.dot_general(lhs, rhs, (((0,), (0,)), ((), ())), preferred_element_type=F32)

    def grad_part(slot, b):
        for n in range(half // tile):
            gp[slot, :, n * tile : (n + 1) * tile] = grad_block(b, n).astype(BF16)

    @pl.when(even)
    def _():
        pl.semaphore_signal(turn, inc=1, device_id=at_layer(above, h), device_id_type=MESH)

    grad_part(0, j_far)
    pl.when(jnp.logical_not(even))(lambda: pl.semaphore_wait(turn, 1))
    send(gp.at[0, low], gl.at[0], s_g, r_gl.at[0], b_right)
    send(gp.at[0, high], gl.at[1], s_g, r_gl.at[1], b_left)
    grad_part(1, j_right)
    send(gp.at[1, high], gr.at[0, high], s_g, r_g, b_right)
    grad_part(2, j_left)
    send(gp.at[2, low], gr.at[1, low], s_g, r_g, b_left)
    for n in range(half // tile):
        gown[:, n * tile : (n + 1) * tile] = grad_block(j, n)
    store_own = pltpu.make_async_copy(gown, own_ref, s_own)
    store_own.start()
    for side_way, (rows, dev) in enumerate(((low, b_right), (high, b_left))):
        wait_bytes(gl.at[side_way], r_gl.at[side_way])
        for n in range(half // tile):
            cols = slice(n * tile, (n + 1) * tile)
            part = gp[1 + side_way, rows, cols].astype(F32) + gl[side_way, :, cols].astype(F32)
            gp[1 + side_way, rows, cols] = part.astype(BF16)
        send(gp.at[1 + side_way, rows], gr.at[side_way, rows], s_g, r_g, dev)
    wait_bytes(gr, r_g)
    store_own.wait()

    wait_bytes(wb.at[pl.ds(0, side - 1)], s_w)
    wait_bytes(hns.at[pl.ds(0, side - 1)], s_hn)
    wait_bytes(hns, s_hp)
    wait_bytes(gp, s_g)
    wait_bytes(dxb, s_out)

    def drain(m, carry):
        wait_bytes(up.at[m, pl.ds(0, side - 1)], s_u.at[m])
        wait_bytes(du.at[m, pl.ds(0, side - 1)], s_d.at[m])
        wait_bytes(pr.at[m, pl.ds(0, side - 1), 0], s_po.at[m])
        wait_bytes(pr.at[m, :, 0], s_pp.at[m])

        @pl.when(first)
        def _():
            wait_bytes(c_oth.at[m], s_t.at[m])

        @pl.when(jnp.logical_not(last))
        def _():
            wait_bytes(dxb.at[m], s_c.at[m, 0])
            wait_bytes(dxb.at[m, 0], s_c.at[m, 1])

        return carry

    lax.fori_loop(0, micro, drain, 0)


def shards(acts, top_cot, weights, gains):
    tokens, width = acts.shape[2], acts.shape[3]
    rows, half = weights.shape[2], weights.shape[3]
    layers = lax.axis_size("section")
    parts = lax.axis_size("dp")
    side = int(round(parts**0.5))
    micro = MICRO
    mb = tokens // micro
    kb = rows * side
    dma = pltpu.SemaphoreType.DMA
    vmem = pl.BlockSpec(memory_space=pltpu.VMEM)
    hbm = pl.BlockSpec(memory_space=pl.ANY)
    own, parts_in, out = pl.pallas_call(
        functools.partial(kernel, micro, side, layers),
        out_shape=(
            jax.ShapeDtypeStruct((rows, half), F32),
            jax.ShapeDtypeStruct((2, rows, half), BF16),
            jax.ShapeDtypeStruct((micro, mb, width), BF16),
        ),
        in_specs=[hbm, hbm, hbm, vmem],
        out_specs=(hbm, hbm, hbm),
        scratch_shapes=[
            pltpu.VMEM((micro, mb, width), BF16),
            pltpu.VMEM((side, micro, mb, kb), BF16),
            pltpu.VMEM((micro, side, 2, mb, kb), BF16),
            pltpu.VMEM((side, rows, half), BF16),
            pltpu.VMEM((micro, side, 2, mb, half), BF16),
            pltpu.VMEM((micro, 2, 2, mb, half), BF16),
            pltpu.VMEM((micro, 2, mb, half), BF16),
            pltpu.VMEM((micro, 2, mb, half), BF16),
            pltpu.VMEM((micro, mb, half), BF16),
            pltpu.VMEM((micro, 2, mb, half), BF16),
            pltpu.VMEM((mb, width), F32),
            pltpu.VMEM((micro, side, 2, mb, half), BF16),
            pltpu.VMEM((micro, side, 2, mb, kb), BF16),
            pltpu.VMEM((micro, 2, side, mb, kb), BF16),
            pltpu.VMEM((side - 1, rows, half), BF16),
            pltpu.VMEM((2, rows // 2, half), BF16),
            pltpu.VMEM((rows, half), F32),
            pltpu.VMEM((micro, mb, 128), F32),
            dma, dma((6,)), dma, dma, dma,
            dma((micro,)), dma((micro,)), dma((micro, 2)),
            dma((micro, 2)), dma((micro, 2)),
            dma((micro,)), dma((micro,)),
            dma((micro,)), dma((micro,)), dma((micro,)),
            dma, dma, dma((2,)), dma,
            dma, dma((micro,)), dma,
            dma((2,)),
            pltpu.SemaphoreType.REGULAR, pltpu.SemaphoreType.REGULAR,
        ],
        compiler_params=pltpu.CompilerParams(
            collective_id=0, has_side_effects=True, vmem_limit_bytes=60 * 1024 * 1024
        ),
        cost_estimate=pl.CostEstimate(
            flops=12 * tokens * width * half, bytes_accessed=8 * rows * half, transcendentals=0
        ),
    )(
        acts.reshape(micro, mb, width),
        top_cot.reshape(micro, mb, width),
        weights.reshape(rows, half),
        gains,
    )
    grad = own + parts_in[0].astype(F32) + parts_in[1].astype(F32)
    return grad[None, None], out.reshape(1, 1, tokens, width)


def solution(mesh):
    return jax.shard_map(
        shards,
        mesh=mesh,
        in_specs=(
            P("dir", "section", "dp", None),
            P("dir", "dp", None),
            P("dir", "section", "dp", None),
            P(),
        ),
        out_specs=(P("dir", "section", "dp", None), P("dir", "section", "dp", None)),
        check_vma=False,
    )
```

```python
import functools

import jax
import jax.numpy as jnp
from jax import lax
from jax.experimental import pallas as pl
from jax.experimental.pallas import tpu as pltpu
from jax.sharding import PartitionSpec as P

MESH = pl.DeviceIdType.MESH
MICRO = 8
F32 = jnp.float32
BF16 = jnp.bfloat16


def wait_bytes(ref, sem):
    pltpu.make_async_copy(ref, ref, sem).wait()


def kernel(
    micro, side, layers,
    x_hbm, top_ref, w_hbm, gains_ref,
    own_ref, gr, out_ref,
    x_ref, hns, hnb, wb, up, ur, ul, c_own, c_oth, dxb, dyn_s, du, pr, pp, gp, gl, gown, scl,
    s_w, r_w, s_hn, s_hp, r_hn, s_u, r_u, r_ul, s_c, r_c, s_d, r_d, s_po, s_pp, r_p, s_g, r_g, r_gl, s_own, s_top, s_t, s_out, s_in, turn, ready,
):
    mb, width = x_ref.shape[1], x_ref.shape[2]
    half = w_hbm.shape[1]
    kc = w_hbm.shape[0]
    kb = kc * side
    chunks = side * side
    h = lax.axis_index("dir")
    place = lax.axis_index("section")
    g = lax.axis_index("dp")
    layer = jnp.where(h == 0, place, layers - 1 - place)
    even = lax.rem(layer, 2) == 0
    gy, gx = lax.div(g, side), lax.rem(g, side)
    i, j = jnp.where(even, gy, gx), jnp.where(even, gx, gy)
    sa = jnp.where(even, side, 1)
    sb = jnp.where(even, 1, side)

    def where_is(l, d, a, b):
        return {"section": jnp.where(d == 0, l, layers - 1 - l), "dir": d, "dp": a * sa + b * sb}

    def at_layer(l, d):
        return {"section": jnp.where(d == 0, l, layers - 1 - l), "dir": d, "dp": g}

    def other(v, step):
        return lax.rem(v + step, side)

    i_right, i_far, i_left = other(i, 1), other(i, 2), other(i, 3)
    j_right, j_far, j_left = other(j, 1), other(j, 2), other(j, 3)
    a_right, a_left = where_is(layer, h, i_right, j), where_is(layer, h, i_left, j)
    b_right, b_left = where_is(layer, h, i, j_right), where_is(layer, h, i, j_left)
    low, high = pl.ds(0, kc // 2), pl.ds(kc // 2, kc // 2)

    def send(src, dst, s, r, to):
        pltpu.make_async_remote_copy(
            src_ref=src, dst_ref=dst, send_sem=s, recv_sem=r, device_id=to, device_id_type=MESH
        ).start()

    below = lax.rem(layer + layers - 1, layers)
    above = lax.rem(layer + 1, layers)
    first = layer == layers - 1
    last = layer == 0

    def chunk_of(q):
        a, b = q // side, q % side
        iq, jq = jnp.where(even, a, b), jnp.where(even, b, a)
        return iq, pl.ds(pl.multiple_of(jq * kc, kc), kc)

    peers = []
    for step in range(1, side):
        peers.append(where_is(layer, h, other(i, step), j))
        peers.append(where_is(layer, h, i, other(j, step)))
    for step in range(side):
        peers.append(where_is(layer, 1 - h, other(i, step), j))
    for l in (below, above):
        for d in (h, 1 - h):
            peers.append(at_layer(l, d))
    barrier = pltpu.get_barrier_semaphore()
    for to in peers:
        pl.semaphore_signal(barrier, inc=1, device_id=to, device_id_type=MESH)
    load_x = pltpu.make_async_copy(x_hbm, x_ref, s_in.at[0])
    load_x.start()
    load_w = pltpu.make_async_copy(w_hbm, wb.at[j], s_in.at[1])
    load_w.start()

    @pl.when(first)
    def _():
        for m in range(micro):
            for n in range(2):
                pltpu.make_async_copy(
                    top_ref.at[m, :, pl.ds(n * half, half)], c_own.at[m, n], s_top
                ).start()

    gain_row = pl.ds(layer, 1)

    def norm_step(m, carry):
        xf = x_ref[m].astype(F32)
        scale = lax.rsqrt(jnp.mean(xf * xf, axis=-1, keepdims=True) + 1e-05)
        scl[m] = jnp.broadcast_to(scale, (mb, 128))
        for q in range(chunks):
            iq, cols = chunk_of(q)
            xq = x_ref[m, :, q * kc : (q + 1) * kc].astype(F32)
            hns[iq, m, :, cols] = (xq * scale * gains_ref[gain_row, q * kc : (q + 1) * kc]).astype(BF16)
        return carry

    load_x.wait()
    lax.fori_loop(0, micro, norm_step, 0)
    load_w.wait()
    pl.semaphore_wait(barrier, len(peers))

    def pass_w(slot, part, sem, to):
        send(wb.at[slot, part], wb.at[slot, part], s_w, r_w.at[sem], to)

    def got_w(slot, part, sem):
        wait_bytes(wb.at[slot, part], r_w.at[sem])

    pass_w(j, low, 0, b_right)
    pass_w(j, high, 2, b_left)
    pass_w(j, high, 1, b_right)
    pass_w(j, low, 3, b_left)

    def relay_w():
        got_w(j_left, low, 0)
        pass_w(j_left, low, 4, b_right)
        got_w(j_right, high, 2)
        pass_w(j_right, high, 5, b_left)

    @pl.when(even)
    def _():
        relay_w()
        pl.semaphore_wait(ready, 1)

    for step in range(side):
        to = other(i, step)
        send(hns.at[to], hnb.at[:, i, h], s_hp, r_hn, where_is(layer, 1 - h, to, j))
        if step:
            send(hns.at[to], hnb.at[:, i, h], s_hn, r_hn, where_is(layer, h, to, j))
        else:
            pltpu.make_async_copy(hns.at[i], hnb.at[:, i, h], r_hn).start()

    @pl.when(first)
    def _():
        wait_bytes(c_own, s_top)
        for m in range(micro):
            send(c_own.at[m, 1 - h], c_oth.at[m], s_t.at[m], r_c.at[m, 1], at_layer(layer, 1 - h))

    pl.when(jnp.logical_not(even))(relay_w)
    got_w(j_left, high, 1)
    got_w(j_right, low, 3)
    got_w(j_far, low, 4)
    got_w(j_far, high, 5)

    @pl.when(jnp.logical_not(even))
    def _():
        pl.semaphore_signal(ready, inc=1, device_id=at_layer(below, h), device_id_type=MESH)

    wait_bytes(hnb, r_hn)

    tile = min(512, half)

    def fwd_step(m):
        rows = hnb[m].reshape(side * 2 * mb, kb)
        for n in range(half // tile):
            cols = slice(n * tile, (n + 1) * tile)
            part = jnp.dot(rows, wb[:, :, cols].reshape(kb, tile), preferred_element_type=F32)
            up[m, :, :, :, cols] = part.astype(BF16).reshape(side, 2, mb, tile)
        send(up.at[m, i_far, 0], ul.at[m, 0], s_u.at[m], r_ul.at[m, 0], a_right)
        send(up.at[m, i_far, 1], ul.at[m, 1], s_u.at[m], r_ul.at[m, 1], a_left)
        send(up.at[m, i_right, 1], ur.at[m, 0, 1], s_u.at[m], r_u.at[m], a_right)
        send(up.at[m, i_left, 0], ur.at[m, 1, 0], s_u.at[m], r_u.at[m], a_left)

    def relay_step(m):
        for r, (to, dev) in enumerate(((i_right, a_right), (i_left, a_left))):
            wait_bytes(ul.at[m, r], r_ul.at[m, r])
            for n in range(half // tile):
                cols = slice(n * tile, (n + 1) * tile)
                part = up[m, to, r, :, cols].astype(F32) + ul[m, r, :, cols].astype(F32)
                up[m, to, r, :, cols] = part.astype(BF16)
            send(up.at[m, to, r], ur.at[m, r, r], s_u.at[m], r_u.at[m], dev)

    def du_step(m):
        wait_bytes(ur.at[m], r_u.at[m])

        @pl.when(jnp.logical_not(first))
        def _():
            wait_bytes(c_own.at[m], r_c.at[m, 0])

        wait_bytes(c_oth.at[m], r_c.at[m, 1])
        for n in range(half // tile):
            cols = slice(n * tile, (n + 1) * tile)
            for mine in range(2):
                r = h if mine else 1 - h
                u = up[m, i, r, :, cols].astype(F32)
                u = u + ur[m, 0, r, :, cols].astype(F32) + ur[m, 1, r, :, cols].astype(F32)
                sig = jax.nn.sigmoid(u)
                slope = sig * (1.0 + u * (1.0 - sig))
                c = c_own[m, h, :, cols] if mine else c_oth[m, :, cols]
                du[m, i, r, :, cols] = (c.astype(F32) * slope).astype(BF16)
        for step in range(1, side):
            to = other(i, step)
            send(du.at[m, i], du.at[m, i], s_d.at[m], r_d.at[m], where_is(layer, h, to, j))

    def prod_step(m):
        wait_bytes(du.at[m, pl.ds(0, side - 1)], r_d.at[m])
        rows = du[m].reshape(side * 2 * mb, half)
        for k in range(side):
            part = lax.dot_general(rows, wb[k], (((1,), (1,)), ((), ())), preferred_element_type=F32)
            pr[m, :, :, :, k * kc : (k + 1) * kc] = part.astype(BF16).reshape(side, 2, mb, kc)
        for step in range(side):
            to = other(i, step)
            send(pr.at[m, to, 1 - h], pp.at[m, h, i], s_pp.at[m], r_p.at[m], where_is(layer, 1 - h, to, j))
            if step:
                send(pr.at[m, to, h], pp.at[m, h, i], s_po.at[m], r_p.at[m], where_is(layer, h, to, j))
            else:
                pltpu.make_async_copy(pr.at[m, i, h], pp.at[m, h, i], r_p.at[m]).start()

    def dx_step(m):
        wait_bytes(pp.at[m], r_p.at[m])
        scale = scl[m][:, :1]
        total = jnp.zeros((mb, kc), F32)
        for q in range(chunks):
            iq, cols = chunk_of(q)
            nat = slice(q * kc, (q + 1) * kc)
            dhn = pp[m, 0, iq, :, cols].astype(F32) + pp[m, 1, iq, :, cols].astype(F32)
            dyn = dhn * gains_ref[gain_row, nat]
            dyn_s[:, nat] = dyn
            total = total + dyn * (x_ref[m, :, nat].astype(F32) * scale)
        mean = jnp.sum(total, axis=-1, keepdims=True) * (1.0 / width)
        per = chunks // 2
        for q in range(chunks):
            nat = slice(q * kc, (q + 1) * kc)
            low = slice((q % per) * kc, (q % per + 1) * kc)
            normed = x_ref[m, :, nat].astype(F32) * scale
            dxn = scale * (dyn_s[:, nat] - normed * mean)
            dxb[m, q // per, :, low] = (c_own[m, q // per, :, low].astype(F32) + dxn).astype(BF16)

        @pl.when(jnp.logical_not(last))
        def _():
            send(dxb.at[m], c_own.at[m], s_c.at[m, 0], r_c.at[m, 0], at_layer(below, h))
            send(dxb.at[m, 1 - h], c_oth.at[m], s_c.at[m, 1], r_c.at[m, 1], at_layer(below, 1 - h))

        for n in range(2):
            pltpu.make_async_copy(dxb.at[m, n], out_ref.at[m, :, pl.ds(n * half, half)], s_out).start()

    lag = 2
    begin = jnp.where(first, lag + 1, micro + lag)

    def step_at(t, carry):
        c = t - begin
        pl.when(t < micro)(lambda: fwd_step(t))
        pl.when((t >= lag) & (t < micro + lag))(lambda: relay_step(t - lag))
        pl.when((c >= 0) & (c < micro))(lambda: du_step(c))
        pl.when((c >= 1) & (c < micro + 1))(lambda: prod_step(c - 1))
        pl.when(c >= 2)(lambda: dx_step(c - 2))
        return carry

    lax.fori_loop(0, begin + micro + 1, step_at, 0)

    pl.when(jnp.logical_not(last))(lambda: dx_step(micro - 1))

    def grad_block(b, n):
        cols = slice(n * tile, (n + 1) * tile)
        lhs = hnb[:, :, :, :, pl.ds(pl.multiple_of(b * kc, kc), kc)].reshape(micro * side * 2 * mb, kc)
        rhs = du[:, :, :, :, cols].reshape(micro * side * 2 * mb, tile)
        return lax.dot_general(lhs, rhs, (((0,), (0,)), ((), ())), preferred_element_type=F32)

    def grad_part(slot, b):
        for n in range(half // tile):
            gp[slot, :, n * tile : (n + 1) * tile] = grad_block(b, n).astype(BF16)

    @pl.when(even)
    def _():
        pl.semaphore_signal(turn, inc=1, device_id=at_layer(above, h), device_id_type=MESH)

    grad_part(0, j_far)
    pl.when(jnp.logical_not(even))(lambda: pl.semaphore_wait(turn, 1))
    send(gp.at[0, low], gl.at[0], s_g, r_gl.at[0], b_right)
    send(gp.at[0, high], gl.at[1], s_g, r_gl.at[1], b_left)
    grad_part(1, j_right)
    send(gp.at[1, high], gr.at[0, high], s_g, r_g, b_right)
    grad_part(2, j_left)
    send(gp.at[2, low], gr.at[1, low], s_g, r_g, b_left)
    pl.when(last)(lambda: dx_step(micro - 1))
    for n in range(half // tile):
        gown[:, n * tile : (n + 1) * tile] = grad_block(j, n)
    store_own = pltpu.make_async_copy(gown, own_ref, s_own)
    store_own.start()
    for side_way, (rows, dev) in enumerate(((low, b_right), (high, b_left))):
        wait_bytes(gl.at[side_way], r_gl.at[side_way])
        for n in range(half // tile):
            cols = slice(n * tile, (n + 1) * tile)
            part = gp[1 + side_way, rows, cols].astype(F32) + gl[side_way, :, cols].astype(F32)
            gp[1 + side_way, rows, cols] = part.astype(BF16)
        send(gp.at[1 + side_way, rows], gr.at[side_way, rows], s_g, r_g, dev)
    wait_bytes(gr, r_g)
    store_own.wait()

    wait_bytes(wb.at[pl.ds(0, side - 1)], s_w)
    wait_bytes(hns.at[pl.ds(0, side - 1)], s_hn)
    wait_bytes(hns, s_hp)
    wait_bytes(gp, s_g)
    wait_bytes(dxb, s_out)

    def drain(m, carry):
        wait_bytes(up.at[m, pl.ds(0, side - 1)], s_u.at[m])
        wait_bytes(du.at[m, pl.ds(0, side - 1)], s_d.at[m])
        wait_bytes(pr.at[m, pl.ds(0, side - 1), 0], s_po.at[m])
        wait_bytes(pr.at[m, :, 0], s_pp.at[m])

        @pl.when(first)
        def _():
            wait_bytes(c_oth.at[m], s_t.at[m])

        @pl.when(jnp.logical_not(last))
        def _():
            wait_bytes(dxb.at[m], s_c.at[m, 0])
            wait_bytes(dxb.at[m, 0], s_c.at[m, 1])

        return carry

    lax.fori_loop(0, micro, drain, 0)


def finish(own_hbm, parts_hbm, out_hbm, grad_hbm, res_hbm, own, parts, out, s_own, s_parts, s_out, s_grad, s_res):
    count = s_own.shape[0]
    rows = own.shape[0] // count
    def at(k):
        return pl.ds(k * rows, rows)
    loads = []
    for k in range(count):
        loads.append((
            pltpu.make_async_copy(own_hbm.at[at(k)], own.at[at(k)], s_own.at[k]),
            pltpu.make_async_copy(parts_hbm.at[:, at(k)], parts.at[:, at(k)], s_parts.at[k]),
        ))
        for copy in loads[-1]:
            copy.start()
    load_out = pltpu.make_async_copy(out_hbm, out, s_out)
    load_out.start()
    stores = []
    for k in range(count):
        for copy in loads[k]:
            copy.wait()
        own[at(k)] = own[at(k)] + parts[0, at(k)].astype(F32) + parts[1, at(k)].astype(F32)
        stores.append(pltpu.make_async_copy(own.at[at(k)], grad_hbm.at[at(k)], s_grad.at[k]))
        stores[-1].start()
    load_out.wait()
    stores.append(pltpu.make_async_copy(out, res_hbm, s_res))
    stores[-1].start()
    for copy in stores:
        copy.wait()


def shards(acts, top_cot, weights, gains):
    tokens, width = acts.shape[2], acts.shape[3]
    rows, half = weights.shape[2], weights.shape[3]
    layers = lax.axis_size("section")
    parts = lax.axis_size("dp")
    side = int(round(parts**0.5))
    micro = MICRO
    mb = tokens // micro
    kb = rows * side
    dma = pltpu.SemaphoreType.DMA
    vmem = pl.BlockSpec(memory_space=pltpu.VMEM)
    hbm = pl.BlockSpec(memory_space=pl.ANY)
    own, parts_in, out = pl.pallas_call(
        functools.partial(kernel, micro, side, layers),
        out_shape=(
            jax.ShapeDtypeStruct((rows, half), F32),
            jax.ShapeDtypeStruct((2, rows, half), BF16),
            jax.ShapeDtypeStruct((micro, mb, width), BF16),
        ),
        in_specs=[hbm, hbm, hbm, vmem],
        out_specs=(hbm, hbm, hbm),
        scratch_shapes=[
            pltpu.VMEM((micro, mb, width), BF16),
            pltpu.VMEM((side, micro, mb, kb), BF16),
            pltpu.VMEM((micro, side, 2, mb, kb), BF16),
            pltpu.VMEM((side, rows, half), BF16),
            pltpu.VMEM((micro, side, 2, mb, half), BF16),
            pltpu.VMEM((micro, 2, 2, mb, half), BF16),
            pltpu.VMEM((micro, 2, mb, half), BF16),
            pltpu.VMEM((micro, 2, mb, half), BF16),
            pltpu.VMEM((micro, mb, half), BF16),
            pltpu.VMEM((micro, 2, mb, half), BF16),
            pltpu.VMEM((mb, width), F32),
            pltpu.VMEM((micro, side, 2, mb, half), BF16),
            pltpu.VMEM((micro, side, 2, mb, kb), BF16),
            pltpu.VMEM((micro, 2, side, mb, kb), BF16),
            pltpu.VMEM((side - 1, rows, half), BF16),
            pltpu.VMEM((2, rows // 2, half), BF16),
            pltpu.VMEM((rows, half), F32),
            pltpu.VMEM((micro, mb, 128), F32),
            dma, dma((6,)), dma, dma, dma,
            dma((micro,)), dma((micro,)), dma((micro, 2)),
            dma((micro, 2)), dma((micro, 2)),
            dma((micro,)), dma((micro,)),
            dma((micro,)), dma((micro,)), dma((micro,)),
            dma, dma, dma((2,)), dma,
            dma, dma((micro,)), dma,
            dma((2,)),
            pltpu.SemaphoreType.REGULAR, pltpu.SemaphoreType.REGULAR,
        ],
        compiler_params=pltpu.CompilerParams(
            collective_id=0, has_side_effects=True, vmem_limit_bytes=60 * 1024 * 1024
        ),
        cost_estimate=pl.CostEstimate(
            flops=12 * tokens * width * half, bytes_accessed=8 * rows * half, transcendentals=0
        ),
    )(
        acts.reshape(micro, mb, width),
        top_cot.reshape(micro, mb, width),
        weights.reshape(rows, half),
        gains,
    )
    count = 4
    grad, out = pl.pallas_call(
        finish,
        out_shape=(
            jax.ShapeDtypeStruct((rows, half), F32),
            jax.ShapeDtypeStruct((micro, mb, width), BF16),
        ),
        in_specs=[hbm, hbm, hbm],
        out_specs=(hbm, hbm),
        scratch_shapes=[
            pltpu.VMEM((rows, half), F32),
            pltpu.VMEM((2, rows, half), BF16),
            pltpu.VMEM((micro, mb, width), BF16),
            dma((count,)), dma((count,)), dma, dma((count,)), dma,
        ],
        compiler_params=pltpu.CompilerParams(vmem_limit_bytes=60 * 1024 * 1024),
        cost_estimate=pl.CostEstimate(flops=2 * rows * half, bytes_accessed=20 * rows * half, transcendentals=0),
    )(own, parts_in, out)
    return grad[None, None], out.reshape(1, 1, tokens, width)


def solution(mesh):
    return jax.shard_map(
        shards,
        mesh=mesh,
        in_specs=(
            P("dir", "section", "dp", None),
            P("dir", "dp", None),
            P("dir", "section", "dp", None),
            P(),
        ),
        out_specs=(P("dir", "section", "dp", None), P("dir", "section", "dp", None)),
        check_vma=False,
    )
```

```python
import functools

import jax
import jax.numpy as jnp
from jax import lax
from jax.experimental import pallas as pl
from jax.experimental.pallas import tpu as pltpu
from jax.sharding import PartitionSpec as P

MESH = pl.DeviceIdType.MESH
MICRO = 8
F32 = jnp.float32
BF16 = jnp.bfloat16


def wait_bytes(ref, sem):
    pltpu.make_async_copy(ref, ref, sem).wait()


def kernel(
    micro, side, layers,
    x_hbm, top_ref, w_hbm, gains_ref,
    own_ref, gr, out_ref,
    x_ref, hns, hnb, wb, up, ur, ul, c_own, c_oth, dxb, dyn_s, du, pr, pp, gp, gl, gown, scl,
    s_w, r_w, s_hn, s_hp, r_hn, s_u, r_u, r_ul, s_c, r_c, s_d, r_d, s_po, s_pp, r_p, s_g, r_g, r_gl, s_own, s_top, s_t, s_out, s_in, turn, ready,
):
    mb, width = x_ref.shape[1], x_ref.shape[2]
    half = w_hbm.shape[1]
    kc = w_hbm.shape[0]
    kb = kc * side
    chunks = side * side
    h = lax.axis_index("dir")
    place = lax.axis_index("section")
    g = lax.axis_index("dp")
    layer = jnp.where(h == 0, place, layers - 1 - place)
    even = lax.rem(layer, 2) == 0
    gy, gx = lax.div(g, side), lax.rem(g, side)
    i, j = jnp.where(even, gy, gx), jnp.where(even, gx, gy)
    sa = jnp.where(even, side, 1)
    sb = jnp.where(even, 1, side)

    def where_is(l, d, a, b):
        return {"section": jnp.where(d == 0, l, layers - 1 - l), "dir": d, "dp": a * sa + b * sb}

    def at_layer(l, d):
        return {"section": jnp.where(d == 0, l, layers - 1 - l), "dir": d, "dp": g}

    def other(v, step):
        return lax.rem(v + step, side)

    i_right, i_far, i_left = other(i, 1), other(i, 2), other(i, 3)
    j_right, j_far, j_left = other(j, 1), other(j, 2), other(j, 3)
    a_right, a_left = where_is(layer, h, i_right, j), where_is(layer, h, i_left, j)
    b_right, b_left = where_is(layer, h, i, j_right), where_is(layer, h, i, j_left)
    low, high = pl.ds(0, kc // 2), pl.ds(kc // 2, kc // 2)

    def send(src, dst, s, r, to):
        pltpu.make_async_remote_copy(
            src_ref=src, dst_ref=dst, send_sem=s, recv_sem=r, device_id=to, device_id_type=MESH
        ).start()

    below = lax.rem(layer + layers - 1, layers)
    above = lax.rem(layer + 1, layers)
    first = layer == layers - 1
    last = layer == 0

    def chunk_of(q):
        a, b = q // side, q % side
        iq, jq = jnp.where(even, a, b), jnp.where(even, b, a)
        return iq, pl.ds(pl.multiple_of(jq * kc, kc), kc)

    peers = []
    for step in range(1, side):
        peers.append(where_is(layer, h, other(i, step), j))
        peers.append(where_is(layer, h, i, other(j, step)))
    for step in range(side):
        peers.append(where_is(layer, 1 - h, other(i, step), j))
    for l in (below, above):
        for d in (h, 1 - h):
            peers.append(at_layer(l, d))
    barrier = pltpu.get_barrier_semaphore()
    for to in peers:
        pl.semaphore_signal(barrier, inc=1, device_id=to, device_id_type=MESH)
    load_x = pltpu.make_async_copy(x_hbm, x_ref, s_in.at[0])
    load_x.start()
    load_w = pltpu.make_async_copy(w_hbm, wb.at[j], s_in.at[1])
    load_w.start()

    @pl.when(first)
    def _():
        for m in range(micro):
            for n in range(2):
                pltpu.make_async_copy(
                    top_ref.at[m, :, pl.ds(n * half, half)], c_own.at[m, n], s_top
                ).start()

    gain_row = pl.ds(layer, 1)

    def norm_step(m, carry):
        xf = x_ref[m].astype(F32)
        scale = lax.rsqrt(jnp.mean(xf * xf, axis=-1, keepdims=True) + 1e-05)
        scl[m] = jnp.broadcast_to(scale, (mb, 128))
        for q in range(chunks):
            iq, cols = chunk_of(q)
            xq = x_ref[m, :, q * kc : (q + 1) * kc].astype(F32)
            hns[iq, m, :, cols] = (xq * scale * gains_ref[gain_row, q * kc : (q + 1) * kc]).astype(BF16)
        return carry

    load_x.wait()
    lax.fori_loop(0, micro, norm_step, 0)
    load_w.wait()
    pl.semaphore_wait(barrier, len(peers))

    def pass_w(slot, part, sem, to):
        send(wb.at[slot, part], wb.at[slot, part], s_w, r_w.at[sem], to)

    def got_w(slot, part, sem):
        wait_bytes(wb.at[slot, part], r_w.at[sem])

    pass_w(j, low, 0, b_right)
    pass_w(j, high, 2, b_left)
    pass_w(j, high, 1, b_right)
    pass_w(j, low, 3, b_left)

    def relay_w():
        got_w(j_left, low, 0)
        pass_w(j_left, low, 4, b_right)
        got_w(j_right, high, 2)
        pass_w(j_right, high, 5, b_left)

    @pl.when(even)
    def _():
        relay_w()
        pl.semaphore_wait(ready, 1)

    for step in range(side):
        to = other(i, step)
        send(hns.at[to], hnb.at[:, i, h], s_hp, r_hn, where_is(layer, 1 - h, to, j))
        if step:
            send(hns.at[to], hnb.at[:, i, h], s_hn, r_hn, where_is(layer, h, to, j))
        else:
            pltpu.make_async_copy(hns.at[i], hnb.at[:, i, h], r_hn).start()

    @pl.when(first)
    def _():
        wait_bytes(c_own, s_top)
        for m in range(micro):
            send(c_own.at[m, 1 - h], c_oth.at[m], s_t.at[m], r_c.at[m, 1], at_layer(layer, 1 - h))

    pl.when(jnp.logical_not(even))(relay_w)
    got_w(j_left, high, 1)
    got_w(j_right, low, 3)
    got_w(j_far, low, 4)
    got_w(j_far, high, 5)

    @pl.when(jnp.logical_not(even))
    def _():
        pl.semaphore_signal(ready, inc=1, device_id=at_layer(below, h), device_id_type=MESH)

    wait_bytes(hnb, r_hn)

    tile = min(512, half)

    def fwd_step(m):
        rows = hnb[m].reshape(side * 2 * mb, kb)
        for n in range(half // tile):
            cols = slice(n * tile, (n + 1) * tile)
            part = jnp.dot(rows, wb[:, :, cols].reshape(kb, tile), preferred_element_type=F32)
            up[m, :, :, :, cols] = part.astype(BF16).reshape(side, 2, mb, tile)
        send(up.at[m, i_far, 0], ul.at[m, 0], s_u.at[m], r_ul.at[m, 0], a_right)
        send(up.at[m, i_far, 1], ul.at[m, 1], s_u.at[m], r_ul.at[m, 1], a_left)
        send(up.at[m, i_right, 1], ur.at[m, 0, 1], s_u.at[m], r_u.at[m], a_right)
        send(up.at[m, i_left, 0], ur.at[m, 1, 0], s_u.at[m], r_u.at[m], a_left)

    def relay_step(m):
        for r, (to, dev) in enumerate(((i_right, a_right), (i_left, a_left))):
            wait_bytes(ul.at[m, r], r_ul.at[m, r])
            for n in range(half // tile):
                cols = slice(n * tile, (n + 1) * tile)
                part = up[m, to, r, :, cols].astype(F32) + ul[m, r, :, cols].astype(F32)
                up[m, to, r, :, cols] = part.astype(BF16)
            send(up.at[m, to, r], ur.at[m, r, r], s_u.at[m], r_u.at[m], dev)

    def du_step(m):
        wait_bytes(ur.at[m], r_u.at[m])

        @pl.when(jnp.logical_not(first))
        def _():
            wait_bytes(c_own.at[m], r_c.at[m, 0])

        wait_bytes(c_oth.at[m], r_c.at[m, 1])
        for n in range(half // tile):
            cols = slice(n * tile, (n + 1) * tile)
            for mine in range(2):
                r = h if mine else 1 - h
                u = up[m, i, r, :, cols].astype(F32)
                u = u + ur[m, 0, r, :, cols].astype(F32) + ur[m, 1, r, :, cols].astype(F32)
                sig = jax.nn.sigmoid(u)
                slope = sig * (1.0 + u * (1.0 - sig))
                c = c_own[m, h, :, cols] if mine else c_oth[m, :, cols]
                du[m, i, r, :, cols] = (c.astype(F32) * slope).astype(BF16)
        for step in (2, 1, 3):
            to = other(i, step)
            send(du.at[m, i], du.at[m, i], s_d.at[m], r_d.at[m], where_is(layer, h, to, j))

    def prod_step(m):
        wait_bytes(du.at[m, pl.ds(0, side - 1)], r_d.at[m])
        rows = du[m].reshape(side * 2 * mb, half)
        for part in range(2):
            some = pl.ds(part * (kb // 2), kb // 2)
            for k in range(part * side // 2, (part + 1) * side // 2):
                prod = lax.dot_general(rows, wb[k], (((1,), (1,)), ((), ())), preferred_element_type=F32)
                pr[m, :, :, :, k * kc : (k + 1) * kc] = prod.astype(BF16).reshape(side, 2, mb, kc)
            for step in (2, 1, 3, 0):
                to = other(i, step)
                send(pr.at[m, to, 1 - h, :, some], pp.at[m, h, i, :, some], s_pp.at[m], r_p.at[m], where_is(layer, 1 - h, to, j))
            for step in (2, 1, 3):
                to = other(i, step)
                send(pr.at[m, to, h, :, some], pp.at[m, h, i, :, some], s_po.at[m], r_p.at[m], where_is(layer, h, to, j))
            pltpu.make_async_copy(pr.at[m, i, h, :, some], pp.at[m, h, i, :, some], r_p.at[m]).start()

    def dx_step(m):
        wait_bytes(pp.at[m], r_p.at[m])
        scale = scl[m][:, :1]
        total = jnp.zeros((mb, kc), F32)
        for q in range(chunks):
            iq, cols = chunk_of(q)
            nat = slice(q * kc, (q + 1) * kc)
            dhn = pp[m, 0, iq, :, cols].astype(F32) + pp[m, 1, iq, :, cols].astype(F32)
            dyn = dhn * gains_ref[gain_row, nat]
            dyn_s[:, nat] = dyn
            total = total + dyn * (x_ref[m, :, nat].astype(F32) * scale)
        mean = jnp.sum(total, axis=-1, keepdims=True) * (1.0 / width)
        per = chunks // 2
        for q in range(chunks):
            nat = slice(q * kc, (q + 1) * kc)
            low = slice((q % per) * kc, (q % per + 1) * kc)
            normed = x_ref[m, :, nat].astype(F32) * scale
            dxn = scale * (dyn_s[:, nat] - normed * mean)
            dxb[m, q // per, :, low] = (c_own[m, q // per, :, low].astype(F32) + dxn).astype(BF16)

        @pl.when(jnp.logical_not(last))
        def _():
            send(dxb.at[m], c_own.at[m], s_c.at[m, 0], r_c.at[m, 0], at_layer(below, h))
            send(dxb.at[m, 1 - h], c_oth.at[m], s_c.at[m, 1], r_c.at[m, 1], at_layer(below, 1 - h))

        for n in range(2):
            pltpu.make_async_copy(dxb.at[m, n], out_ref.at[m, :, pl.ds(n * half, half)], s_out).start()

    lag = 2
    begin = jnp.where(first, lag + 1, micro + lag)

    def step_at(t, carry):
        c = t - begin
        pl.when(t < micro)(lambda: fwd_step(t))
        pl.when((t >= lag) & (t < micro + lag))(lambda: relay_step(t - lag))
        pl.when((c >= 0) & (c < micro))(lambda: du_step(c))
        pl.when((c >= 1) & (c < micro + 1))(lambda: prod_step(c - 1))
        pl.when(c >= 2)(lambda: dx_step(c - 2))
        return carry

    lax.fori_loop(0, begin + micro + 1, step_at, 0)

    pl.when(jnp.logical_not(last))(lambda: dx_step(micro - 1))

    def grad_block(b, n, part=None):
        cols = slice(n * tile, (n + 1) * tile)
        size = kc if part is None else kc // 2
        start = pl.multiple_of(b * kc + (part or 0) * size, size)
        lhs = hnb[:, :, :, :, pl.ds(start, size)].reshape(micro * side * 2 * mb, size)
        rhs = du[:, :, :, :, cols].reshape(micro * side * 2 * mb, tile)
        return lax.dot_general(lhs, rhs, (((0,), (0,)), ((), ())), preferred_element_type=F32)

    def grad_part(slot, b):
        for n in range(half // tile):
            gp[slot, :, n * tile : (n + 1) * tile] = grad_block(b, n).astype(BF16)

    @pl.when(even)
    def _():
        pl.semaphore_signal(turn, inc=1, device_id=at_layer(above, h), device_id_type=MESH)

    def grad_half(b, part):
        for n in range(half // tile):
            gp[0, part * kc // 2 : (part + 1) * kc // 2, n * tile : (n + 1) * tile] = grad_block(b, n, part).astype(BF16)

    grad_half(j_far, 0)
    pl.when(jnp.logical_not(even))(lambda: pl.semaphore_wait(turn, 1))
    send(gp.at[0, low], gl.at[0], s_g, r_gl.at[0], b_right)
    grad_half(j_far, 1)
    send(gp.at[0, high], gl.at[1], s_g, r_gl.at[1], b_left)
    grad_part(1, j_right)
    send(gp.at[1, high], gr.at[0, high], s_g, r_g, b_right)
    grad_part(2, j_left)
    send(gp.at[2, low], gr.at[1, low], s_g, r_g, b_left)
    pl.when(last)(lambda: dx_step(micro - 1))
    for n in range(half // tile):
        gown[:, n * tile : (n + 1) * tile] = grad_block(j, n)
    store_own = pltpu.make_async_copy(gown, own_ref, s_own)
    store_own.start()
    for side_way, (rows, dev) in enumerate(((low, b_right), (high, b_left))):
        wait_bytes(gl.at[side_way], r_gl.at[side_way])
        for n in range(half // tile):
            cols = slice(n * tile, (n + 1) * tile)
            part = gp[1 + side_way, rows, cols].astype(F32) + gl[side_way, :, cols].astype(F32)
            gp[1 + side_way, rows, cols] = part.astype(BF16)
        send(gp.at[1 + side_way, rows], gr.at[side_way, rows], s_g, r_g, dev)
    wait_bytes(gr, r_g)
    store_own.wait()

    wait_bytes(wb.at[pl.ds(0, side - 1)], s_w)
    wait_bytes(hns.at[pl.ds(0, side - 1)], s_hn)
    wait_bytes(hns, s_hp)
    wait_bytes(gp, s_g)
    wait_bytes(dxb, s_out)

    def drain(m, carry):
        wait_bytes(up.at[m, pl.ds(0, side - 1)], s_u.at[m])
        wait_bytes(du.at[m, pl.ds(0, side - 1)], s_d.at[m])
        wait_bytes(pr.at[m, pl.ds(0, side - 1), 0], s_po.at[m])
        wait_bytes(pr.at[m, :, 0], s_pp.at[m])

        @pl.when(first)
        def _():
            wait_bytes(c_oth.at[m], s_t.at[m])

        @pl.when(jnp.logical_not(last))
        def _():
            wait_bytes(dxb.at[m], s_c.at[m, 0])
            wait_bytes(dxb.at[m, 0], s_c.at[m, 1])

        return carry

    lax.fori_loop(0, micro, drain, 0)


def finish(own_hbm, parts_hbm, out_hbm, grad_hbm, res_hbm, own, parts, out, s_own, s_parts, s_out, s_grad, s_res):
    count = s_own.shape[0]
    rows = own.shape[0] // count
    def at(k):
        return pl.ds(k * rows, rows)
    loads = []
    for k in range(count):
        loads.append((
            pltpu.make_async_copy(own_hbm.at[at(k)], own.at[at(k)], s_own.at[k]),
            pltpu.make_async_copy(parts_hbm.at[:, at(k)], parts.at[:, at(k)], s_parts.at[k]),
        ))
        for copy in loads[-1]:
            copy.start()
    load_out = pltpu.make_async_copy(out_hbm, out, s_out)
    load_out.start()
    stores = []
    for k in range(count):
        for copy in loads[k]:
            copy.wait()
        own[at(k)] = own[at(k)] + parts[0, at(k)].astype(F32) + parts[1, at(k)].astype(F32)
        stores.append(pltpu.make_async_copy(own.at[at(k)], grad_hbm.at[at(k)], s_grad.at[k]))
        stores[-1].start()
    load_out.wait()
    stores.append(pltpu.make_async_copy(out, res_hbm, s_res))
    stores[-1].start()
    for copy in stores:
        copy.wait()


def shards(acts, top_cot, weights, gains):
    tokens, width = acts.shape[2], acts.shape[3]
    rows, half = weights.shape[2], weights.shape[3]
    layers = lax.axis_size("section")
    parts = lax.axis_size("dp")
    side = int(round(parts**0.5))
    micro = MICRO
    mb = tokens // micro
    kb = rows * side
    dma = pltpu.SemaphoreType.DMA
    vmem = pl.BlockSpec(memory_space=pltpu.VMEM)
    hbm = pl.BlockSpec(memory_space=pl.ANY)
    own, parts_in, out = pl.pallas_call(
        functools.partial(kernel, micro, side, layers),
        out_shape=(
            jax.ShapeDtypeStruct((rows, half), F32),
            jax.ShapeDtypeStruct((2, rows, half), BF16),
            jax.ShapeDtypeStruct((micro, mb, width), BF16),
        ),
        in_specs=[hbm, hbm, hbm, vmem],
        out_specs=(hbm, hbm, hbm),
        scratch_shapes=[
            pltpu.VMEM((micro, mb, width), BF16),
            pltpu.VMEM((side, micro, mb, kb), BF16),
            pltpu.VMEM((micro, side, 2, mb, kb), BF16),
            pltpu.VMEM((side, rows, half), BF16),
            pltpu.VMEM((micro, side, 2, mb, half), BF16),
            pltpu.VMEM((micro, 2, 2, mb, half), BF16),
            pltpu.VMEM((micro, 2, mb, half), BF16),
            pltpu.VMEM((micro, 2, mb, half), BF16),
            pltpu.VMEM((micro, mb, half), BF16),
            pltpu.VMEM((micro, 2, mb, half), BF16),
            pltpu.VMEM((mb, width), F32),
            pltpu.VMEM((micro, side, 2, mb, half), BF16),
            pltpu.VMEM((micro, side, 2, mb, kb), BF16),
            pltpu.VMEM((micro, 2, side, mb, kb), BF16),
            pltpu.VMEM((side - 1, rows, half), BF16),
            pltpu.VMEM((2, rows // 2, half), BF16),
            pltpu.VMEM((rows, half), F32),
            pltpu.VMEM((micro, mb, 128), F32),
            dma, dma((6,)), dma, dma, dma,
            dma((micro,)), dma((micro,)), dma((micro, 2)),
            dma((micro, 2)), dma((micro, 2)),
            dma((micro,)), dma((micro,)),
            dma((micro,)), dma((micro,)), dma((micro,)),
            dma, dma, dma((2,)), dma,
            dma, dma((micro,)), dma,
            dma((2,)),
            pltpu.SemaphoreType.REGULAR, pltpu.SemaphoreType.REGULAR,
        ],
        compiler_params=pltpu.CompilerParams(
            collective_id=0, has_side_effects=True, vmem_limit_bytes=60 * 1024 * 1024
        ),
        cost_estimate=pl.CostEstimate(
            flops=12 * tokens * width * half, bytes_accessed=8 * rows * half, transcendentals=0
        ),
    )(
        acts.reshape(micro, mb, width),
        top_cot.reshape(micro, mb, width),
        weights.reshape(rows, half),
        gains,
    )
    count = 4
    grad, out = pl.pallas_call(
        finish,
        out_shape=(
            jax.ShapeDtypeStruct((rows, half), F32),
            jax.ShapeDtypeStruct((micro, mb, width), BF16),
        ),
        in_specs=[hbm, hbm, hbm],
        out_specs=(hbm, hbm),
        scratch_shapes=[
            pltpu.VMEM((rows, half), F32),
            pltpu.VMEM((2, rows, half), BF16),
            pltpu.VMEM((micro, mb, width), BF16),
            dma((count,)), dma((count,)), dma, dma((count,)), dma,
        ],
        compiler_params=pltpu.CompilerParams(vmem_limit_bytes=60 * 1024 * 1024),
        cost_estimate=pl.CostEstimate(flops=2 * rows * half, bytes_accessed=20 * rows * half, transcendentals=0),
    )(own, parts_in, out)
    return grad[None, None], out.reshape(1, 1, tokens, width)


def solution(mesh):
    return jax.shard_map(
        shards,
        mesh=mesh,
        in_specs=(
            P("dir", "section", "dp", None),
            P("dir", "dp", None),
            P("dir", "section", "dp", None),
            P(),
        ),
        out_specs=(P("dir", "section", "dp", None), P("dir", "section", "dp", None)),
        check_vma=False,
    )
```

```python
import functools

import jax
import jax.numpy as jnp
from jax import lax
from jax.experimental import pallas as pl
from jax.experimental.pallas import tpu as pltpu
from jax.sharding import PartitionSpec as P

MESH = pl.DeviceIdType.MESH
MICRO = 8
F32 = jnp.float32
BF16 = jnp.bfloat16


def wait_bytes(ref, sem):
    pltpu.make_async_copy(ref, ref, sem).wait()


def kernel(
    micro, side, layers,
    x_hbm, top_ref, w_hbm, gains_ref,
    own_ref, gr, out_ref,
    x_ref, hns, hnb, wb, up, ur, ul, c_own, c_oth, dxb, dyn_s, du, pr, pp, gp, gl, gown, scl,
    s_w, r_w, s_hn, s_hp, r_hn, s_u, r_u, r_ul, s_c, r_c, s_d, r_d, s_po, s_pp, r_p, s_g, r_g, r_gl, s_own, s_top, s_t, s_out, s_in, turn, ready,
):
    mb, width = x_ref.shape[1], x_ref.shape[2]
    half = w_hbm.shape[1]
    kc = w_hbm.shape[0]
    kb = kc * side
    chunks = side * side
    h = lax.axis_index("dir")
    place = lax.axis_index("section")
    g = lax.axis_index("dp")
    layer = jnp.where(h == 0, place, layers - 1 - place)
    even = lax.rem(layer, 2) == 0
    gy, gx = lax.div(g, side), lax.rem(g, side)
    i, j = jnp.where(even, gy, gx), jnp.where(even, gx, gy)
    sa = jnp.where(even, side, 1)
    sb = jnp.where(even, 1, side)

    def where_is(l, d, a, b):
        return {"section": jnp.where(d == 0, l, layers - 1 - l), "dir": d, "dp": a * sa + b * sb}

    def at_layer(l, d):
        return {"section": jnp.where(d == 0, l, layers - 1 - l), "dir": d, "dp": g}

    def other(v, step):
        return lax.rem(v + step, side)

    i_right, i_far, i_left = other(i, 1), other(i, 2), other(i, 3)
    j_right, j_far, j_left = other(j, 1), other(j, 2), other(j, 3)
    a_right, a_left = where_is(layer, h, i_right, j), where_is(layer, h, i_left, j)
    b_right, b_left = where_is(layer, h, i, j_right), where_is(layer, h, i, j_left)
    low, high = pl.ds(0, kc // 2), pl.ds(kc // 2, kc // 2)

    def send(src, dst, s, r, to):
        pltpu.make_async_remote_copy(
            src_ref=src, dst_ref=dst, send_sem=s, recv_sem=r, device_id=to, device_id_type=MESH
        ).start()

    below = lax.rem(layer + layers - 1, layers)
    above = lax.rem(layer + 1, layers)
    first = layer == layers - 1
    last = layer == 0

    def chunk_of(q):
        a, b = q // side, q % side
        iq, jq = jnp.where(even, a, b), jnp.where(even, b, a)
        return iq, pl.ds(pl.multiple_of(jq * kc, kc), kc)

    peers = []
    for step in range(1, side):
        peers.append(where_is(layer, h, other(i, step), j))
        peers.append(where_is(layer, h, i, other(j, step)))
    for step in range(side):
        peers.append(where_is(layer, 1 - h, other(i, step), j))
    for l in (below, above):
        for d in (h, 1 - h):
            peers.append(at_layer(l, d))
    barrier = pltpu.get_barrier_semaphore()
    for to in peers:
        pl.semaphore_signal(barrier, inc=1, device_id=to, device_id_type=MESH)
    load_x = pltpu.make_async_copy(x_hbm, x_ref, s_in.at[0])
    load_x.start()
    load_w = pltpu.make_async_copy(w_hbm, wb.at[j], s_in.at[1])
    load_w.start()

    @pl.when(first)
    def _():
        for m in range(micro):
            for n in range(2):
                pltpu.make_async_copy(
                    top_ref.at[m, :, pl.ds(n * half, half)], c_own.at[m, n], s_top
                ).start()

    gain_row = pl.ds(layer, 1)

    def norm_step(m, carry):
        xf = x_ref[m].astype(F32)
        scale = lax.rsqrt(jnp.mean(xf * xf, axis=-1, keepdims=True) + 1e-05)
        scl[m] = jnp.broadcast_to(scale, (mb, 128))
        for q in range(chunks):
            iq, cols = chunk_of(q)
            xq = x_ref[m, :, q * kc : (q + 1) * kc].astype(F32)
            hns[iq, m, :, cols] = (xq * scale * gains_ref[gain_row, q * kc : (q + 1) * kc]).astype(BF16)
        return carry

    load_x.wait()
    lax.fori_loop(0, micro, norm_step, 0)
    load_w.wait()
    pl.semaphore_wait(barrier, len(peers))

    def pass_w(slot, part, sem, to):
        send(wb.at[slot, part], wb.at[slot, part], s_w, r_w.at[sem], to)

    def got_w(slot, part, sem):
        wait_bytes(wb.at[slot, part], r_w.at[sem])

    pass_w(j, low, 0, b_right)
    pass_w(j, high, 2, b_left)
    pass_w(j, high, 1, b_right)
    pass_w(j, low, 3, b_left)

    def relay_w():
        got_w(j_left, low, 0)
        pass_w(j_left, low, 4, b_right)
        got_w(j_right, high, 2)
        pass_w(j_right, high, 5, b_left)

    @pl.when(even)
    def _():
        relay_w()
        pl.semaphore_wait(ready, 1)

    for step in range(side):
        to = other(i, step)
        send(hns.at[to], hnb.at[:, i, h], s_hp, r_hn, where_is(layer, 1 - h, to, j))
        if step:
            send(hns.at[to], hnb.at[:, i, h], s_hn, r_hn, where_is(layer, h, to, j))
        else:
            pltpu.make_async_copy(hns.at[i], hnb.at[:, i, h], r_hn).start()

    @pl.when(first)
    def _():
        wait_bytes(c_own, s_top)
        for m in range(micro):
            send(c_own.at[m, 1 - h], c_oth.at[m], s_t.at[m], r_c.at[m, 1], at_layer(layer, 1 - h))

    pl.when(jnp.logical_not(even))(relay_w)
    got_w(j_left, high, 1)
    got_w(j_right, low, 3)
    got_w(j_far, low, 4)
    got_w(j_far, high, 5)

    @pl.when(jnp.logical_not(even))
    def _():
        pl.semaphore_signal(ready, inc=1, device_id=at_layer(below, h), device_id_type=MESH)

    wait_bytes(hnb, r_hn)

    tile = min(512, half)

    def fwd_step(m):
        rows = hnb[m].reshape(side * 2 * mb, kb)
        for n in range(half // tile):
            cols = slice(n * tile, (n + 1) * tile)
            part = jnp.dot(rows, wb[:, :, cols].reshape(kb, tile), preferred_element_type=F32)
            up[m, :, :, :, cols] = part.astype(BF16).reshape(side, 2, mb, tile)
        send(up.at[m, i_far, 0], ul.at[m, 0], s_u.at[m], r_ul.at[m, 0], a_right)
        send(up.at[m, i_far, 1], ul.at[m, 1], s_u.at[m], r_ul.at[m, 1], a_left)
        send(up.at[m, i_right, 1], ur.at[m, 0, 1], s_u.at[m], r_u.at[m], a_right)
        send(up.at[m, i_left, 0], ur.at[m, 1, 0], s_u.at[m], r_u.at[m], a_left)

    def relay_step(m):
        for r, (to, dev) in enumerate(((i_right, a_right), (i_left, a_left))):
            wait_bytes(ul.at[m, r], r_ul.at[m, r])
            for n in range(half // tile):
                cols = slice(n * tile, (n + 1) * tile)
                part = up[m, to, r, :, cols].astype(F32) + ul[m, r, :, cols].astype(F32)
                up[m, to, r, :, cols] = part.astype(BF16)
            send(up.at[m, to, r], ur.at[m, r, r], s_u.at[m], r_u.at[m], dev)

    def du_step(m):
        wait_bytes(ur.at[m], r_u.at[m])

        @pl.when(jnp.logical_not(first))
        def _():
            wait_bytes(c_own.at[m], r_c.at[m, 0])

        wait_bytes(c_oth.at[m], r_c.at[m, 1])
        for n in range(half // tile):
            cols = slice(n * tile, (n + 1) * tile)
            for mine in range(2):
                r = h if mine else 1 - h
                u = up[m, i, r, :, cols].astype(F32)
                u = u + ur[m, 0, r, :, cols].astype(F32) + ur[m, 1, r, :, cols].astype(F32)
                sig = jax.nn.sigmoid(u)
                slope = sig * (1.0 + u * (1.0 - sig))
                c = c_own[m, h, :, cols] if mine else c_oth[m, :, cols]
                du[m, i, r, :, cols] = (c.astype(F32) * slope).astype(BF16)
        for step in (2, 1, 3):
            to = other(i, step)
            send(du.at[m, i], du.at[m, i], s_d.at[m], r_d.at[m], where_is(layer, h, to, j))

    def prod_step(m):
        wait_bytes(du.at[m, pl.ds(0, side - 1)], r_d.at[m])
        rows = du[m].reshape(side * 2 * mb, half)
        for part in range(2):
            some = pl.ds(part * (kb // 2), kb // 2)
            for k in range(part * side // 2, (part + 1) * side // 2):
                prod = lax.dot_general(rows, wb[k], (((1,), (1,)), ((), ())), preferred_element_type=F32)
                pr[m, :, :, :, k * kc : (k + 1) * kc] = prod.astype(BF16).reshape(side, 2, mb, kc)
            for step in (2, 1, 3, 0):
                to = other(i, step)
                send(pr.at[m, to, 1 - h, :, some], pp.at[m, h, i, :, some], s_pp.at[m], r_p.at[m], where_is(layer, 1 - h, to, j))
            for step in (2, 1, 3):
                to = other(i, step)
                send(pr.at[m, to, h, :, some], pp.at[m, h, i, :, some], s_po.at[m], r_p.at[m], where_is(layer, h, to, j))
            pltpu.make_async_copy(pr.at[m, i, h, :, some], pp.at[m, h, i, :, some], r_p.at[m]).start()

    def dx_step(m):
        wait_bytes(pp.at[m], r_p.at[m])
        scale = scl[m][:, :1]
        total = jnp.zeros((mb, kc), F32)
        for q in range(chunks):
            iq, cols = chunk_of(q)
            nat = slice(q * kc, (q + 1) * kc)
            dhn = pp[m, 0, iq, :, cols].astype(F32) + pp[m, 1, iq, :, cols].astype(F32)
            dyn = dhn * gains_ref[gain_row, nat]
            dyn_s[:, nat] = dyn
            total = total + dyn * (x_ref[m, :, nat].astype(F32) * scale)
        mean = jnp.sum(total, axis=-1, keepdims=True) * (1.0 / width)
        per = chunks // 2
        for q in range(chunks):
            nat = slice(q * kc, (q + 1) * kc)
            low = slice((q % per) * kc, (q % per + 1) * kc)
            normed = x_ref[m, :, nat].astype(F32) * scale
            dxn = scale * (dyn_s[:, nat] - normed * mean)
            dxb[m, q // per, :, low] = (c_own[m, q // per, :, low].astype(F32) + dxn).astype(BF16)

        @pl.when(jnp.logical_not(last))
        def _():
            send(dxb.at[m, 1 - h], c_oth.at[m], s_c.at[m, 1], r_c.at[m, 1], at_layer(below, 1 - h))
            for n in range(2):
                send(dxb.at[m, n], c_own.at[m, n], s_c.at[m, 0], r_c.at[m, 0], at_layer(below, h))

        for n in range(2):
            pltpu.make_async_copy(dxb.at[m, n], out_ref.at[m, :, pl.ds(n * half, half)], s_out).start()

    lag = 2
    begin = jnp.where(first, lag + 1, micro + lag)

    def step_at(t, carry):
        c = t - begin
        pl.when(t < micro)(lambda: fwd_step(t))
        pl.when((t >= lag) & (t < micro + lag))(lambda: relay_step(t - lag))
        pl.when((c >= 0) & (c < micro))(lambda: du_step(c))
        pl.when((c >= 1) & (c < micro + 1))(lambda: prod_step(c - 1))
        pl.when(c >= 2)(lambda: dx_step(c - 2))
        return carry

    lax.fori_loop(0, begin + micro + 1, step_at, 0)

    pl.when(jnp.logical_not(last))(lambda: dx_step(micro - 1))

    def grad_block(b, n, part=None):
        cols = slice(n * tile, (n + 1) * tile)
        size = kc if part is None else kc // 2
        start = pl.multiple_of(b * kc + (part or 0) * size, size)
        lhs = hnb[:, :, :, :, pl.ds(start, size)].reshape(micro * side * 2 * mb, size)
        rhs = du[:, :, :, :, cols].reshape(micro * side * 2 * mb, tile)
        return lax.dot_general(lhs, rhs, (((0,), (0,)), ((), ())), preferred_element_type=F32)

    def grad_part(slot, b):
        for n in range(half // tile):
            gp[slot, :, n * tile : (n + 1) * tile] = grad_block(b, n).astype(BF16)

    @pl.when(even)
    def _():
        pl.semaphore_signal(turn, inc=1, device_id=at_layer(above, h), device_id_type=MESH)

    def grad_half(b, part):
        for n in range(half // tile):
            gp[0, part * kc // 2 : (part + 1) * kc // 2, n * tile : (n + 1) * tile] = grad_block(b, n, part).astype(BF16)

    grad_half(j_far, 0)
    pl.when(jnp.logical_not(even))(lambda: pl.semaphore_wait(turn, 1))
    send(gp.at[0, low], gl.at[0], s_g, r_gl.at[0], b_right)
    grad_half(j_far, 1)
    send(gp.at[0, high], gl.at[1], s_g, r_gl.at[1], b_left)
    grad_part(1, j_right)
    send(gp.at[1, high], gr.at[0, high], s_g, r_g, b_right)
    grad_part(2, j_left)
    send(gp.at[2, low], gr.at[1, low], s_g, r_g, b_left)
    pl.when(last)(lambda: dx_step(micro - 1))
    for n in range(half // tile):
        gown[:, n * tile : (n + 1) * tile] = grad_block(j, n)
    store_own = pltpu.make_async_copy(gown, own_ref, s_own)
    store_own.start()
    for side_way, (rows, dev) in enumerate(((low, b_right), (high, b_left))):
        wait_bytes(gl.at[side_way], r_gl.at[side_way])
        for n in range(half // tile):
            cols = slice(n * tile, (n + 1) * tile)
            part = gp[1 + side_way, rows, cols].astype(F32) + gl[side_way, :, cols].astype(F32)
            gp[1 + side_way, rows, cols] = part.astype(BF16)
        send(gp.at[1 + side_way, rows], gr.at[side_way, rows], s_g, r_g, dev)
    wait_bytes(gr, r_g)
    store_own.wait()

    wait_bytes(wb.at[pl.ds(0, side - 1)], s_w)
    wait_bytes(hns.at[pl.ds(0, side - 1)], s_hn)
    wait_bytes(hns, s_hp)
    wait_bytes(gp, s_g)
    wait_bytes(dxb, s_out)

    def drain(m, carry):
        wait_bytes(up.at[m, pl.ds(0, side - 1)], s_u.at[m])
        wait_bytes(du.at[m, pl.ds(0, side - 1)], s_d.at[m])
        wait_bytes(pr.at[m, pl.ds(0, side - 1), 0], s_po.at[m])
        wait_bytes(pr.at[m, :, 0], s_pp.at[m])

        @pl.when(first)
        def _():
            wait_bytes(c_oth.at[m], s_t.at[m])

        @pl.when(jnp.logical_not(last))
        def _():
            wait_bytes(dxb.at[m], s_c.at[m, 0])
            wait_bytes(dxb.at[m, 0], s_c.at[m, 1])

        return carry

    lax.fori_loop(0, micro, drain, 0)


def finish(own_hbm, parts_hbm, out_hbm, grad_hbm, res_hbm, own, parts, out, s_own, s_parts, s_out, s_grad, s_res):
    count = s_own.shape[0]
    rows = own.shape[0] // count
    def at(k):
        return pl.ds(k * rows, rows)
    loads = []
    for k in range(count):
        loads.append((
            pltpu.make_async_copy(own_hbm.at[at(k)], own.at[at(k)], s_own.at[k]),
            pltpu.make_async_copy(parts_hbm.at[:, at(k)], parts.at[:, at(k)], s_parts.at[k]),
        ))
        for copy in loads[-1]:
            copy.start()
    load_out = pltpu.make_async_copy(out_hbm, out, s_out)
    load_out.start()
    stores = []
    for k in range(count):
        for copy in loads[k]:
            copy.wait()
        own[at(k)] = own[at(k)] + parts[0, at(k)].astype(F32) + parts[1, at(k)].astype(F32)
        stores.append(pltpu.make_async_copy(own.at[at(k)], grad_hbm.at[at(k)], s_grad.at[k]))
        stores[-1].start()
    load_out.wait()
    stores.append(pltpu.make_async_copy(out, res_hbm, s_res))
    stores[-1].start()
    for copy in stores:
        copy.wait()


def shards(acts, top_cot, weights, gains):
    tokens, width = acts.shape[2], acts.shape[3]
    rows, half = weights.shape[2], weights.shape[3]
    layers = lax.axis_size("section")
    parts = lax.axis_size("dp")
    side = int(round(parts**0.5))
    micro = MICRO
    mb = tokens // micro
    kb = rows * side
    dma = pltpu.SemaphoreType.DMA
    vmem = pl.BlockSpec(memory_space=pltpu.VMEM)
    hbm = pl.BlockSpec(memory_space=pl.ANY)
    own, parts_in, out = pl.pallas_call(
        functools.partial(kernel, micro, side, layers),
        out_shape=(
            jax.ShapeDtypeStruct((rows, half), F32),
            jax.ShapeDtypeStruct((2, rows, half), BF16),
            jax.ShapeDtypeStruct((micro, mb, width), BF16),
        ),
        in_specs=[hbm, hbm, hbm, vmem],
        out_specs=(hbm, hbm, hbm),
        scratch_shapes=[
            pltpu.VMEM((micro, mb, width), BF16),
            pltpu.VMEM((side, micro, mb, kb), BF16),
            pltpu.VMEM((micro, side, 2, mb, kb), BF16),
            pltpu.VMEM((side, rows, half), BF16),
            pltpu.VMEM((micro, side, 2, mb, half), BF16),
            pltpu.VMEM((micro, 2, 2, mb, half), BF16),
            pltpu.VMEM((micro, 2, mb, half), BF16),
            pltpu.VMEM((micro, 2, mb, half), BF16),
            pltpu.VMEM((micro, mb, half), BF16),
            pltpu.VMEM((micro, 2, mb, half), BF16),
            pltpu.VMEM((mb, width), F32),
            pltpu.VMEM((micro, side, 2, mb, half), BF16),
            pltpu.VMEM((micro, side, 2, mb, kb), BF16),
            pltpu.VMEM((micro, 2, side, mb, kb), BF16),
            pltpu.VMEM((side - 1, rows, half), BF16),
            pltpu.VMEM((2, rows // 2, half), BF16),
            pltpu.VMEM((rows, half), F32),
            pltpu.VMEM((micro, mb, 128), F32),
            dma, dma((6,)), dma, dma, dma,
            dma((micro,)), dma((micro,)), dma((micro, 2)),
            dma((micro, 2)), dma((micro, 2)),
            dma((micro,)), dma((micro,)),
            dma((micro,)), dma((micro,)), dma((micro,)),
            dma, dma, dma((2,)), dma,
            dma, dma((micro,)), dma,
            dma((2,)),
            pltpu.SemaphoreType.REGULAR, pltpu.SemaphoreType.REGULAR,
        ],
        compiler_params=pltpu.CompilerParams(
            collective_id=0, has_side_effects=True, vmem_limit_bytes=60 * 1024 * 1024
        ),
        cost_estimate=pl.CostEstimate(
            flops=12 * tokens * width * half, bytes_accessed=8 * rows * half, transcendentals=0
        ),
    )(
        acts.reshape(micro, mb, width),
        top_cot.reshape(micro, mb, width),
        weights.reshape(rows, half),
        gains,
    )
    count = 4
    grad, out = pl.pallas_call(
        finish,
        out_shape=(
            jax.ShapeDtypeStruct((rows, half), F32),
            jax.ShapeDtypeStruct((micro, mb, width), BF16),
        ),
        in_specs=[hbm, hbm, hbm],
        out_specs=(hbm, hbm),
        scratch_shapes=[
            pltpu.VMEM((rows, half), F32),
            pltpu.VMEM((2, rows, half), BF16),
            pltpu.VMEM((micro, mb, width), BF16),
            dma((count,)), dma((count,)), dma, dma((count,)), dma,
        ],
        compiler_params=pltpu.CompilerParams(vmem_limit_bytes=60 * 1024 * 1024),
        cost_estimate=pl.CostEstimate(flops=2 * rows * half, bytes_accessed=20 * rows * half, transcendentals=0),
    )(own, parts_in, out)
    return grad[None, None], out.reshape(1, 1, tokens, width)


def solution(mesh):
    return jax.shard_map(
        shards,
        mesh=mesh,
        in_specs=(
            P("dir", "section", "dp", None),
            P("dir", "dp", None),
            P("dir", "section", "dp", None),
            P(),
        ),
        out_specs=(P("dir", "section", "dp", None), P("dir", "section", "dp", None)),
        check_vma=False,
    )
```

```python
import functools

import jax
import jax.numpy as jnp
from jax import lax
from jax.experimental import pallas as pl
from jax.experimental.pallas import tpu as pltpu
from jax.sharding import PartitionSpec as P

MESH = pl.DeviceIdType.MESH
MICRO = 8
F32 = jnp.float32
BF16 = jnp.bfloat16


def wait_bytes(ref, sem):
    pltpu.make_async_copy(ref, ref, sem).wait()


def kernel(
    micro, side, layers,
    x_hbm, top_ref, w_hbm, gains_ref,
    own_ref, gr, out_ref,
    x_ref, hns, hnb, wb, up, ur, ul, c_own, c_oth, dxb, dyn_s, du, pr, pp, gp, gl, gown, scl,
    s_w, r_w, s_hn, s_hp, r_hn, s_u, r_u, r_ul, s_c, r_c, s_d, r_d, s_po, s_pp, r_p, s_g, r_g, r_gl, s_own, s_top, s_t, s_out, s_in, turn, ready,
):
    mb, width = x_ref.shape[1], x_ref.shape[2]
    half = w_hbm.shape[1]
    kc = w_hbm.shape[0]
    kb = kc * side
    chunks = side * side
    h = lax.axis_index("dir")
    place = lax.axis_index("section")
    g = lax.axis_index("dp")
    layer = jnp.where(h == 0, place, layers - 1 - place)
    even = lax.rem(layer, 2) == 0
    gy, gx = lax.div(g, side), lax.rem(g, side)
    i, j = jnp.where(even, gy, gx), jnp.where(even, gx, gy)
    sa = jnp.where(even, side, 1)
    sb = jnp.where(even, 1, side)

    def where_is(l, d, a, b):
        return {"section": jnp.where(d == 0, l, layers - 1 - l), "dir": d, "dp": a * sa + b * sb}

    def at_layer(l, d):
        return {"section": jnp.where(d == 0, l, layers - 1 - l), "dir": d, "dp": g}

    def other(v, step):
        return lax.rem(v + step, side)

    i_right, i_far, i_left = other(i, 1), other(i, 2), other(i, 3)
    j_right, j_far, j_left = other(j, 1), other(j, 2), other(j, 3)
    a_right, a_left = where_is(layer, h, i_right, j), where_is(layer, h, i_left, j)
    b_right, b_left = where_is(layer, h, i, j_right), where_is(layer, h, i, j_left)
    low, high = pl.ds(0, kc // 2), pl.ds(kc // 2, kc // 2)

    def send(src, dst, s, r, to):
        pltpu.make_async_remote_copy(
            src_ref=src, dst_ref=dst, send_sem=s, recv_sem=r, device_id=to, device_id_type=MESH
        ).start()

    below = lax.rem(layer + layers - 1, layers)
    above = lax.rem(layer + 1, layers)
    first = layer == layers - 1
    last = layer == 0

    def chunk_of(q):
        a, b = q // side, q % side
        iq, jq = jnp.where(even, a, b), jnp.where(even, b, a)
        return iq, pl.ds(pl.multiple_of(jq * kc, kc), kc)

    peers = []
    for step in range(1, side):
        peers.append(where_is(layer, h, other(i, step), j))
        peers.append(where_is(layer, h, i, other(j, step)))
    for step in range(side):
        peers.append(where_is(layer, 1 - h, other(i, step), j))
    for l in (below, above):
        for d in (h, 1 - h):
            peers.append(at_layer(l, d))
    barrier = pltpu.get_barrier_semaphore()
    for to in peers:
        pl.semaphore_signal(barrier, inc=1, device_id=to, device_id_type=MESH)
    load_x = pltpu.make_async_copy(x_hbm, x_ref, s_in.at[0])
    load_x.start()
    load_w = pltpu.make_async_copy(w_hbm, wb.at[j], s_in.at[1])
    load_w.start()

    @pl.when(first)
    def _():
        for m in range(micro):
            for n in range(2):
                pltpu.make_async_copy(
                    top_ref.at[m, :, pl.ds(n * half, half)], c_own.at[m, n], s_top
                ).start()

    gain_row = pl.ds(layer, 1)

    def norm_step(m, carry):
        xf = x_ref[m].astype(F32)
        scale = lax.rsqrt(jnp.mean(xf * xf, axis=-1, keepdims=True) + 1e-05)
        scl[m] = jnp.broadcast_to(scale, (mb, 128))
        for q in range(chunks):
            iq, cols = chunk_of(q)
            xq = x_ref[m, :, q * kc : (q + 1) * kc].astype(F32)
            hns[iq, m, :, cols] = (xq * scale * gains_ref[gain_row, q * kc : (q + 1) * kc]).astype(BF16)
        return carry

    load_x.wait()
    lax.fori_loop(0, micro, norm_step, 0)
    load_w.wait()
    pl.semaphore_wait(barrier, len(peers))

    def pass_w(slot, part, sem, to):
        send(wb.at[slot, part], wb.at[slot, part], s_w, r_w.at[sem], to)

    def got_w(slot, part, sem):
        wait_bytes(wb.at[slot, part], r_w.at[sem])

    pass_w(j, low, 0, b_right)
    pass_w(j, high, 2, b_left)
    pass_w(j, high, 1, b_right)
    pass_w(j, low, 3, b_left)

    def relay_w():
        got_w(j_left, low, 0)
        pass_w(j_left, low, 4, b_right)
        got_w(j_right, high, 2)
        pass_w(j_right, high, 5, b_left)

    @pl.when(even)
    def _():
        relay_w()
        pl.semaphore_wait(ready, 1)

    for step in range(side):
        to = other(i, step)
        send(hns.at[to], hnb.at[:, i, h], s_hp, r_hn, where_is(layer, 1 - h, to, j))
        if step:
            send(hns.at[to], hnb.at[:, i, h], s_hn, r_hn, where_is(layer, h, to, j))
        else:
            pltpu.make_async_copy(hns.at[i], hnb.at[:, i, h], r_hn).start()

    @pl.when(first)
    def _():
        wait_bytes(c_own, s_top)
        for m in range(micro):
            send(c_own.at[m, 1 - h], c_oth.at[m], s_t.at[m], r_c.at[m, 1], at_layer(layer, 1 - h))

    pl.when(jnp.logical_not(even))(relay_w)
    got_w(j_left, high, 1)
    got_w(j_right, low, 3)
    got_w(j_far, low, 4)
    got_w(j_far, high, 5)

    @pl.when(jnp.logical_not(even))
    def _():
        pl.semaphore_signal(ready, inc=1, device_id=at_layer(below, h), device_id_type=MESH)

    wait_bytes(hnb, r_hn)

    tile = min(512, half)

    def fwd_step(m):
        rows = hnb[m].reshape(side * 2 * mb, kb)
        for n in range(half // tile):
            cols = slice(n * tile, (n + 1) * tile)
            part = jnp.dot(rows, wb[:, :, cols].reshape(kb, tile), preferred_element_type=F32)
            up[m, :, :, :, cols] = part.astype(BF16).reshape(side, 2, mb, tile)
        send(up.at[m, i_far, 0], ul.at[m, 0], s_u.at[m], r_ul.at[m, 0], a_right)
        send(up.at[m, i_far, 1], ul.at[m, 1], s_u.at[m], r_ul.at[m, 1], a_left)
        send(up.at[m, i_right, 1], ur.at[m, 0, 1], s_u.at[m], r_u.at[m], a_right)
        send(up.at[m, i_left, 0], ur.at[m, 1, 0], s_u.at[m], r_u.at[m], a_left)

    def relay_step(m):
        for r, (to, dev) in enumerate(((i_right, a_right), (i_left, a_left))):
            wait_bytes(ul.at[m, r], r_ul.at[m, r])
            for n in range(half // tile):
                cols = slice(n * tile, (n + 1) * tile)
                part = up[m, to, r, :, cols].astype(F32) + ul[m, r, :, cols].astype(F32)
                up[m, to, r, :, cols] = part.astype(BF16)
            send(up.at[m, to, r], ur.at[m, r, r], s_u.at[m], r_u.at[m], dev)

    def du_step(m):
        wait_bytes(ur.at[m], r_u.at[m])

        @pl.when(jnp.logical_not(first))
        def _():
            wait_bytes(c_own.at[m], r_c.at[m, 0])

        wait_bytes(c_oth.at[m], r_c.at[m, 1])
        for n in range(half // tile):
            cols = slice(n * tile, (n + 1) * tile)
            for mine in range(2):
                r = h if mine else 1 - h
                u = up[m, i, r, :, cols].astype(F32)
                u = u + ur[m, 0, r, :, cols].astype(F32) + ur[m, 1, r, :, cols].astype(F32)
                sig = jax.nn.sigmoid(u)
                slope = sig * (1.0 + u * (1.0 - sig))
                c = c_own[m, h, :, cols] if mine else c_oth[m, :, cols]
                du[m, i, r, :, cols] = (c.astype(F32) * slope).astype(BF16)
        for step in (2, 1, 3):
            to = other(i, step)
            send(du.at[m, i], du.at[m, i], s_d.at[m], r_d.at[m], where_is(layer, h, to, j))

    def prod_step(m):
        wait_bytes(du.at[m, pl.ds(0, side - 1)], r_d.at[m])
        rows = du[m].reshape(side * 2 * mb, half)
        for part in range(2):
            some = pl.ds(part * (kb // 2), kb // 2)
            for k in range(part * side // 2, (part + 1) * side // 2):
                prod = lax.dot_general(rows, wb[k], (((1,), (1,)), ((), ())), preferred_element_type=F32)
                pr[m, :, :, :, k * kc : (k + 1) * kc] = prod.astype(BF16).reshape(side, 2, mb, kc)
            for step in (2, 1, 3, 0):
                to = other(i, step)
                send(pr.at[m, to, 1 - h, :, some], pp.at[m, h, i, :, some], s_pp.at[m], r_p.at[m], where_is(layer, 1 - h, to, j))
            for step in (2, 1, 3):
                to = other(i, step)
                send(pr.at[m, to, h, :, some], pp.at[m, h, i, :, some], s_po.at[m], r_p.at[m], where_is(layer, h, to, j))
            pltpu.make_async_copy(pr.at[m, i, h, :, some], pp.at[m, h, i, :, some], r_p.at[m]).start()

    def dx_step(m):
        wait_bytes(pp.at[m], r_p.at[m])
        scale = scl[m][:, :1]
        total = jnp.zeros((mb, kc), F32)
        for q in range(chunks):
            iq, cols = chunk_of(q)
            nat = slice(q * kc, (q + 1) * kc)
            dhn = pp[m, 0, iq, :, cols].astype(F32) + pp[m, 1, iq, :, cols].astype(F32)
            dyn = dhn * gains_ref[gain_row, nat]
            dyn_s[:, nat] = dyn
            total = total + dyn * (x_ref[m, :, nat].astype(F32) * scale)
        mean = jnp.sum(total, axis=-1, keepdims=True) * (1.0 / width)
        per = chunks // 2
        for q in range(chunks):
            nat = slice(q * kc, (q + 1) * kc)
            low = slice((q % per) * kc, (q % per + 1) * kc)
            normed = x_ref[m, :, nat].astype(F32) * scale
            dxn = scale * (dyn_s[:, nat] - normed * mean)
            dxb[m, q // per, :, low] = (c_own[m, q // per, :, low].astype(F32) + dxn).astype(BF16)

        @pl.when(jnp.logical_not(last))
        def _():
            for n in range(2):
                some = pl.ds(n * (half // 2), half // 2)
                send(dxb.at[m, 1 - h, :, some], c_oth.at[m, :, some], s_c.at[m, 1], r_c.at[m, 1], at_layer(below, 1 - h))
            for n in range(2):
                send(dxb.at[m, n], c_own.at[m, n], s_c.at[m, 0], r_c.at[m, 0], at_layer(below, h))

        for n in range(2):
            pltpu.make_async_copy(dxb.at[m, n], out_ref.at[m, :, pl.ds(n * half, half)], s_out).start()

    lag = 2
    begin = jnp.where(first, lag + 1, micro + lag)

    def step_at(t, carry):
        c = t - begin
        pl.when(t < micro)(lambda: fwd_step(t))
        pl.when((t >= lag) & (t < micro + lag))(lambda: relay_step(t - lag))
        pl.when((c >= 0) & (c < micro))(lambda: du_step(c))
        pl.when((c >= 1) & (c < micro + 1))(lambda: prod_step(c - 1))
        pl.when(c >= 2)(lambda: dx_step(c - 2))
        return carry

    lax.fori_loop(0, begin + micro + 1, step_at, 0)

    pl.when(jnp.logical_not(last))(lambda: dx_step(micro - 1))

    def grad_block(b, n, part=None):
        cols = slice(n * tile, (n + 1) * tile)
        size = kc if part is None else kc // 2
        start = pl.multiple_of(b * kc + (part or 0) * size, size)
        lhs = hnb[:, :, :, :, pl.ds(start, size)].reshape(micro * side * 2 * mb, size)
        rhs = du[:, :, :, :, cols].reshape(micro * side * 2 * mb, tile)
        return lax.dot_general(lhs, rhs, (((0,), (0,)), ((), ())), preferred_element_type=F32)

    def grad_part(slot, b):
        for n in range(half // tile):
            gp[slot, :, n * tile : (n + 1) * tile] = grad_block(b, n).astype(BF16)

    @pl.when(even)
    def _():
        pl.semaphore_signal(turn, inc=1, device_id=at_layer(above, h), device_id_type=MESH)

    def grad_half(b, part):
        for n in range(half // tile):
            gp[0, part * kc // 2 : (part + 1) * kc // 2, n * tile : (n + 1) * tile] = grad_block(b, n, part).astype(BF16)

    grad_half(j_far, 0)
    pl.when(jnp.logical_not(even))(lambda: pl.semaphore_wait(turn, 1))
    send(gp.at[0, low], gl.at[0], s_g, r_gl.at[0], b_right)
    grad_half(j_far, 1)
    send(gp.at[0, high], gl.at[1], s_g, r_gl.at[1], b_left)
    grad_part(1, j_right)
    send(gp.at[1, high], gr.at[0, high], s_g, r_g, b_right)
    grad_part(2, j_left)
    send(gp.at[2, low], gr.at[1, low], s_g, r_g, b_left)
    pl.when(last)(lambda: dx_step(micro - 1))
    for n in range(half // tile):
        gown[:, n * tile : (n + 1) * tile] = grad_block(j, n)
    store_own = pltpu.make_async_copy(gown, own_ref, s_own)
    store_own.start()
    for side_way, (rows, dev) in enumerate(((low, b_right), (high, b_left))):
        wait_bytes(gl.at[side_way], r_gl.at[side_way])
        for n in range(half // tile):
            cols = slice(n * tile, (n + 1) * tile)
            part = gp[1 + side_way, rows, cols].astype(F32) + gl[side_way, :, cols].astype(F32)
            gp[1 + side_way, rows, cols] = part.astype(BF16)
        send(gp.at[1 + side_way, rows], gr.at[side_way, rows], s_g, r_g, dev)
    wait_bytes(gr, r_g)
    store_own.wait()

    wait_bytes(wb.at[pl.ds(0, side - 1)], s_w)
    wait_bytes(hns.at[pl.ds(0, side - 1)], s_hn)
    wait_bytes(hns, s_hp)
    wait_bytes(gp, s_g)
    wait_bytes(dxb, s_out)

    def drain(m, carry):
        wait_bytes(up.at[m, pl.ds(0, side - 1)], s_u.at[m])
        wait_bytes(du.at[m, pl.ds(0, side - 1)], s_d.at[m])
        wait_bytes(pr.at[m, pl.ds(0, side - 1), 0], s_po.at[m])
        wait_bytes(pr.at[m, :, 0], s_pp.at[m])

        @pl.when(first)
        def _():
            wait_bytes(c_oth.at[m], s_t.at[m])

        @pl.when(jnp.logical_not(last))
        def _():
            wait_bytes(dxb.at[m], s_c.at[m, 0])
            wait_bytes(dxb.at[m, 0], s_c.at[m, 1])

        return carry

    lax.fori_loop(0, micro, drain, 0)


def finish(own_hbm, parts_hbm, out_hbm, grad_hbm, res_hbm, own, parts, out, s_own, s_parts, s_out, s_grad, s_res):
    count = s_own.shape[0]
    rows = own.shape[0] // count
    def at(k):
        return pl.ds(k * rows, rows)
    loads = []
    for k in range(count):
        loads.append((
            pltpu.make_async_copy(own_hbm.at[at(k)], own.at[at(k)], s_own.at[k]),
            pltpu.make_async_copy(parts_hbm.at[:, at(k)], parts.at[:, at(k)], s_parts.at[k]),
        ))
        for copy in loads[-1]:
            copy.start()
    load_out = pltpu.make_async_copy(out_hbm, out, s_out)
    load_out.start()
    stores = []
    for k in range(count):
        for copy in loads[k]:
            copy.wait()
        own[at(k)] = own[at(k)] + parts[0, at(k)].astype(F32) + parts[1, at(k)].astype(F32)
        stores.append(pltpu.make_async_copy(own.at[at(k)], grad_hbm.at[at(k)], s_grad.at[k]))
        stores[-1].start()
    load_out.wait()
    stores.append(pltpu.make_async_copy(out, res_hbm, s_res))
    stores[-1].start()
    for copy in stores:
        copy.wait()


def shards(acts, top_cot, weights, gains):
    tokens, width = acts.shape[2], acts.shape[3]
    rows, half = weights.shape[2], weights.shape[3]
    layers = lax.axis_size("section")
    parts = lax.axis_size("dp")
    side = int(round(parts**0.5))
    micro = MICRO
    mb = tokens // micro
    kb = rows * side
    dma = pltpu.SemaphoreType.DMA
    vmem = pl.BlockSpec(memory_space=pltpu.VMEM)
    hbm = pl.BlockSpec(memory_space=pl.ANY)
    own, parts_in, out = pl.pallas_call(
        functools.partial(kernel, micro, side, layers),
        out_shape=(
            jax.ShapeDtypeStruct((rows, half), F32),
            jax.ShapeDtypeStruct((2, rows, half), BF16),
            jax.ShapeDtypeStruct((micro, mb, width), BF16),
        ),
        in_specs=[hbm, hbm, hbm, vmem],
        out_specs=(hbm, hbm, hbm),
        scratch_shapes=[
            pltpu.VMEM((micro, mb, width), BF16),
            pltpu.VMEM((side, micro, mb, kb), BF16),
            pltpu.VMEM((micro, side, 2, mb, kb), BF16),
            pltpu.VMEM((side, rows, half), BF16),
            pltpu.VMEM((micro, side, 2, mb, half), BF16),
            pltpu.VMEM((micro, 2, 2, mb, half), BF16),
            pltpu.VMEM((micro, 2, mb, half), BF16),
            pltpu.VMEM((micro, 2, mb, half), BF16),
            pltpu.VMEM((micro, mb, half), BF16),
            pltpu.VMEM((micro, 2, mb, half), BF16),
            pltpu.VMEM((mb, width), F32),
            pltpu.VMEM((micro, side, 2, mb, half), BF16),
            pltpu.VMEM((micro, side, 2, mb, kb), BF16),
            pltpu.VMEM((micro, 2, side, mb, kb), BF16),
            pltpu.VMEM((side - 1, rows, half), BF16),
            pltpu.VMEM((2, rows // 2, half), BF16),
            pltpu.VMEM((rows, half), F32),
            pltpu.VMEM((micro, mb, 128), F32),
            dma, dma((6,)), dma, dma, dma,
            dma((micro,)), dma((micro,)), dma((micro, 2)),
            dma((micro, 2)), dma((micro, 2)),
            dma((micro,)), dma((micro,)),
            dma((micro,)), dma((micro,)), dma((micro,)),
            dma, dma, dma((2,)), dma,
            dma, dma((micro,)), dma,
            dma((2,)),
            pltpu.SemaphoreType.REGULAR, pltpu.SemaphoreType.REGULAR,
        ],
        compiler_params=pltpu.CompilerParams(
            collective_id=0, has_side_effects=True, vmem_limit_bytes=60 * 1024 * 1024
        ),
        cost_estimate=pl.CostEstimate(
            flops=12 * tokens * width * half, bytes_accessed=8 * rows * half, transcendentals=0
        ),
    )(
        acts.reshape(micro, mb, width),
        top_cot.reshape(micro, mb, width),
        weights.reshape(rows, half),
        gains,
    )
    count = 4
    grad, out = pl.pallas_call(
        finish,
        out_shape=(
            jax.ShapeDtypeStruct((rows, half), F32),
            jax.ShapeDtypeStruct((micro, mb, width), BF16),
        ),
        in_specs=[hbm, hbm, hbm],
        out_specs=(hbm, hbm),
        scratch_shapes=[
            pltpu.VMEM((rows, half), F32),
            pltpu.VMEM((2, rows, half), BF16),
            pltpu.VMEM((micro, mb, width), BF16),
            dma((count,)), dma((count,)), dma, dma((count,)), dma,
        ],
        compiler_params=pltpu.CompilerParams(vmem_limit_bytes=60 * 1024 * 1024),
        cost_estimate=pl.CostEstimate(flops=2 * rows * half, bytes_accessed=20 * rows * half, transcendentals=0),
    )(own, parts_in, out)
    return grad[None, None], out.reshape(1, 1, tokens, width)


def solution(mesh):
    return jax.shard_map(
        shards,
        mesh=mesh,
        in_specs=(
            P("dir", "section", "dp", None),
            P("dir", "dp", None),
            P("dir", "section", "dp", None),
            P(),
        ),
        out_specs=(P("dir", "section", "dp", None), P("dir", "section", "dp", None)),
        check_vma=False,
    )
```
